128 devices in a mesh: outer: 4 (over z_lo, core), inner: 32 (over z_hi, y, x).
Axes of the slice: x: 4, y: 4, z: 4 (z_hi: 2, z_lo: 2; z = z_hi * 2 + z_lo), core: 2. Of those that a mesh axis runs over, the one named last changes fastest.
Arguments:
- vertex: float32 [524288, 128], P(('outer', 'inner')), may hold values from -1.75 to 1.75
- context: float32 [262144, 128], P(('outer', 'inner')), may hold values from -1.75 to 1.75
- tile_count: int32 [512], P(('outer', 'inner')), may hold values from 1 to 8, as said below
- tile_vert: int32 [512, 8], P(('outer', 'inner')), may hold values from 0 to 15
- tile_context: int32 [512, 8], P(('outer', 'inner')), may hold values from 0 to 7
- positives: int32 [512, 8, 256], P(('outer', 'inner')), may hold values from 0 to 255
- negatives: int32 [512, 8, 4, 256], P(('outer', 'inner')), may hold values from 0 to 255
Outputs:
- vertex_out: float32 [524288, 128], P(('outer', 'inner'))
- context_out: float32 [262144, 128], P(('outer', 'inner'))
The draws below stay inside these ranges and needn't reach their ends.
Inputs may be any that keep to these rules, and one draw needn't show every extreme that they name: `tile_count`: every entry is at least 1, and in every tour step some device has all 8 slots live.
All inputs are finite; a program needn't handle non-finite values.
Results may differ from the reference program's by a relative error of at most 0.0003.
Values sent between devices are 32-bit elements; how exact they have to be, the bound alone decides.
No kernel may reach another device: no remote copies, remote signals or barrier semaphores. Data moves between devices by JAX's collectives and lax.ppermute only.
A program may use at most 64 MiB of HBM per device.

```python
import jax
import jax.numpy as jnp
from jax import lax

D = 128
TILE = 256
VROWS = 4096
CROWS = 2048
STEPS = 4
SLOTS = 8
NEG = 4
LISTS = 512
VTOTAL = 524288
CTOTAL = 262144
N_OUTER = 4
N_INNER = 32


def draw_tile_count(key, part):
    members = LISTS // STEPS
    counts = jax.random.randint(key, (members, STEPS), 1, SLOTS)
    chosen = jax.random.randint(jax.random.fold_in(key, 7), (STEPS,), 0, members)
    counts = counts.at[chosen, jnp.arange(STEPS)].set(SLOTS)
    return counts.reshape(LISTS).astype(jnp.int32)


def with_ends(entries, own_key, least, largest):
    dims = entries.shape
    spot = [jax.random.randint(jax.random.fold_in(own_key, axis), (), 0, dims[axis]) for axis in range(len(dims))]
    entries = entries.at[tuple(spot)].set(least)
    longest = dims.index(max(dims))
    spot[longest] = (spot[longest] + 1) % dims[longest]
    return entries.at[tuple(spot)].set(largest)


def levels(own_key, dims, split, smallest, top_value):
    def one(axis_at, parts):
        heights = jax.random.uniform(jax.random.fold_in(jax.random.fold_in(own_key, 6), axis_at), (parts,), jnp.float32, smallest / len(split), top_value / len(split))
        return jnp.repeat(jnp.exp(heights), dims[axis_at] // parts).reshape((-1,) + (1,) * (len(dims) - axis_at - 1))

    level = one(*split[0])
    for cut in split[1:]:
        level = level * one(*cut)
    return level


def centred(key, extent, spread, most, split=(), kind=jnp.bfloat16):
    gain = levels(key, extent, split, -0.22, 0.18) if split else 1.0
    entries = jax.random.normal(key, extent, jnp.float32) * spread * gain
    return jnp.minimum(jnp.maximum(entries, -most), most).astype(kind)


def setup_inputs(seed: int = 0) -> dict:
    key_of = jax.random.split(jax.random.key(seed), 8)
    return {
        "vertex": centred(key_of[0], (VTOTAL, D), 0.3, 1.75, ((0, 128),), jnp.float32),
        "context": centred(key_of[1], (CTOTAL, D), 0.3, 1.75, ((0, 128),), jnp.float32),
        "tile_count": draw_tile_count(jax.random.fold_in(key_of[7], 71), 0),
        "tile_vert": with_ends(jax.random.randint(key_of[3], (LISTS, SLOTS), 0, VROWS // TILE), jax.random.fold_in(key_of[3], 1), 0, (VROWS // TILE) - 1).astype(jnp.int32),
        "tile_context": with_ends(jax.random.randint(key_of[4], (LISTS, SLOTS), 0, CROWS // TILE), jax.random.fold_in(key_of[4], 1), 0, (CROWS // TILE) - 1).astype(jnp.int32),
        "positives": with_ends(jax.random.randint(key_of[5], (LISTS, SLOTS, TILE), 0, TILE), jax.random.fold_in(key_of[5], 1), 0, TILE - 1).astype(jnp.int32),
        "negatives": with_ends(jax.random.randint(key_of[6], (LISTS, SLOTS, NEG, TILE), 0, TILE), jax.random.fold_in(key_of[6], 1), 0, TILE - 1).astype(jnp.int32),
    }


learn_rate = 0.5


def train_rows(visiting, resident, count, tile_vert, tile_context, positives, negatives):
    slots = tile_vert.shape[0]
    width = visiting.shape[1]
    offsets = jnp.arange(TILE, dtype=jnp.int32)
    row_index = tile_vert[:, None] * TILE + offsets[None, :]
    pos_index = tile_context[:, None] * TILE + positives
    neg_index = tile_context[:, None, None] * TILE + negatives
    live = (jnp.arange(slots, dtype=jnp.int32) < count).astype(jnp.float32)
    anchor = visiting[row_index]
    pos_rows = resident[pos_index]
    neg_rows = resident[neg_index]
    pos_score = jnp.sum(anchor * pos_rows, -1)
    neg_score = jnp.sum(anchor[:, None] * neg_rows, -1)
    pos_grad = (jax.nn.sigmoid(pos_score) - 1.0) * live[:, None]
    neg_grad = jax.nn.sigmoid(neg_score) * live[:, None, None]
    vert_delta = pos_grad[..., None] * pos_rows + jnp.sum(neg_grad[..., None] * neg_rows, 1)
    vert_total = jnp.zeros_like(visiting).at[row_index.reshape(-1)].add(vert_delta.reshape(-1, width))
    context_total = jnp.zeros_like(resident).at[pos_index.reshape(-1)].add((pos_grad[..., None] * anchor).reshape(-1, width))
    context_total = context_total.at[neg_index.reshape(-1)].add((neg_grad[..., None] * anchor[:, None]).reshape(-1, width))
    return visiting - learn_rate * vert_total, resident - learn_rate * context_total


def apply_lists(operands):
    return train_rows(*operands)


def reference(vertex, context, tile_count, tile_vert, tile_context, positives, negatives):
    members = N_OUTER * N_INNER
    visiting = vertex.reshape(members, VROWS, D)
    resident = context.reshape(members, CROWS, D)
    counts = tile_count.reshape(members, STEPS)
    vert_lists = tile_vert.reshape(members, STEPS, SLOTS)
    context_lists = tile_context.reshape(members, STEPS, SLOTS)
    pos_lists = positives.reshape(members, STEPS, SLOTS, TILE)
    neg_lists = negatives.reshape(members, STEPS, SLOTS, NEG, TILE)
    for number in range(STEPS):
        visiting, resident = lax.map(apply_lists, (visiting, resident, counts[:, number], vert_lists[:, number], context_lists[:, number], pos_lists[:, number], neg_lists[:, number]))
        if number + 1 < STEPS:
            visiting = jnp.roll(visiting.reshape(N_OUTER, N_INNER, VROWS, D), 1, axis=1).reshape(members, VROWS, D)
    visiting = jnp.roll(visiting.reshape(N_OUTER, N_INNER, VROWS, D), 1, axis=0)
    return visiting.reshape(VTOTAL, D), resident.reshape(CTOTAL, D)
```

```python
import jax
import jax.numpy as jnp
from jax import lax
from jax.experimental import pallas as pl
from jax.experimental.pallas import tpu as pltpu
from jax.sharding import PartitionSpec as P

TILE = 256
HALF = 8
NEG = 4
AXES = ("outer", "inner")
META = 40
LISTED = 48


def route(groups, members, even, odd):
    pairs = []
    for o in range(groups):
        for i in range(members):
            move = even if o % 2 == 0 else odd
            if move is None:
                continue
            to = ((o + move[0]) % groups) * members + (i + move[1]) % members
            pairs.append((o * members + i, to))
    return pairs


def pack_kernel(count, vert, ctx, positives, negatives, *packed):
    lane = lax.broadcasted_iota(jnp.int32, (8, 128), 1)
    for s, out in enumerate(packed):
        out[0:8, :] = positives[s]
        for t in range(8):
            out[8 + NEG * t : 8 + NEG * t + NEG, :] = negatives[s, t]
        meta = jnp.zeros((8, 128), jnp.int32)
        for t in range(8):
            meta = jnp.where(lane == t, vert[s, t], meta)
            meta = jnp.where(lane == 8 + t, ctx[s, t], meta)
        meta = jnp.where(lane == 16, count[s], meta)
        out[META:LISTED, 0:128] = meta
        out[META:LISTED, 128:256] = meta


def halves(x):
    high = x.astype(jnp.bfloat16)
    return high, (x - high.astype(jnp.float32)).astype(jnp.bfloat16)


def dot(a, b, dims):
    return lax.dot_general(a, b, (dims, ((), ())), preferred_element_type=jnp.float32)


def slot_update(v, c, listed, t):
    v_hi, v_lo = halves(v)
    c_hi, c_lo = halves(c)
    c_both = jnp.concatenate([c_hi, c_lo], axis=1)
    v_both = jnp.concatenate([v_hi, v_lo], axis=1)
    scores = dot(c_both, jnp.concatenate([v_hi, v_hi], axis=1), ((1,), (1,)))
    scores = scores + dot(c_hi, v_lo, ((1,), (1,)))
    column = lax.broadcasted_iota(jnp.int32, (TILE, TILE), 0)
    at_pos = listed[pl.ds(t, 1), :] == column
    scale = jnp.where(at_pos, -0.25, 0.0)
    for k in range(NEG):
        scale = scale + jnp.where(listed[pl.ds(8 + NEG * t + k, 1), :] == column, -0.25, 0.0)
    grad = scale * jnp.tanh(0.5 * scores) + (scale + jnp.where(at_pos, 0.5, 0.0))
    g_hi, g_lo = halves(grad)
    dc = dot(g_hi, v_both, ((1,), (0,)))
    dc = dc[:, :128] + dc[:, 128:] + dot(g_lo, v_hi, ((1,), (0,)))
    dv = dot(g_hi, c_both, ((0,), (0,)))
    dv = dv[:, :128] + dv[:, 128:] + dot(g_lo, c_hi, ((0,), (0,)))
    return dv, dc


def step_kernel(first, last, *refs):
    if first:
        vertex, context, listed_in, *refs = refs
    else:
        x, y, z, listed_in, *refs = refs
    if last:
        vertex_out, context_out, *refs = refs
    else:
        x_out, y_out, z_out, *refs = refs
    old, new, listed, meta, sems = refs
    odd = lax.rem(lax.axis_index("outer"), 2)
    v0 = 16 * odd
    c0 = 16 - 16 * odd

    def part(at):
        return pl.ds(at, HALF)

    rows = pltpu.make_async_copy(listed_in, listed, sems.at[0])
    heads = pltpu.make_async_copy(listed_in.at[META:LISTED, 0:128], meta, sems.at[1])
    if first:
        sources = [
            (vertex.at[part(0)], part(v0)),
            (vertex.at[part(HALF)], part(HALF)),
            (context, part(c0)),
        ]
    else:
        sources = [(x, part(0)), (y, part(HALF)), (z, part(16))]
    loads = [
        pltpu.make_async_copy(source, old.at[to], sems.at[2 + n])
        for n, (source, to) in enumerate(sources)
    ]
    heads.start()
    rows.start()
    for load in loads:
        load.start()
    heads.wait()
    rows.wait()
    for load in loads:
        load.wait()

    def fill(n, carry):
        new[n] = old[n]
        return carry

    lax.fori_loop(0, 24, fill, 0)

    def slot(t, carry):
        tile = meta[0, t]
        vi = tile + jnp.where(tile < HALF, v0, 0)
        ci = meta[0, 8 + t] + c0
        dv, dc = slot_update(old[vi], old[ci], listed, t)
        new[vi] += dv
        new[ci] += dc
        return carry

    lax.fori_loop(0, meta[0, 16], slot, 0)

    if last:
        targets = [
            (part(v0), vertex_out.at[part(0)]),
            (part(HALF), vertex_out.at[part(HALF)]),
            (part(c0), context_out),
        ]
    else:
        targets = [(part(0), x_out), (part(HALF), y_out), (part(16), z_out)]
    stores = [
        pltpu.make_async_copy(new.at[source], to, sems.at[5 + n])
        for n, (source, to) in enumerate(targets)
    ]
    for store in stores:
        store.start()
    for store in stores:
        store.wait()


def pack(count, vert, ctx, positives, negatives):
    steps = vert.shape[0]
    smem = pl.BlockSpec(memory_space=pltpu.SMEM)
    vmem = pl.BlockSpec(memory_space=pltpu.VMEM)
    return pl.pallas_call(
        pack_kernel,
        out_shape=[jax.ShapeDtypeStruct((LISTED, TILE), jnp.int32)] * steps,
        in_specs=[smem, smem, smem, vmem, vmem],
        out_specs=[vmem] * steps,
    )(count, vert, ctx, positives, negatives)


def train(first, last, operands):
    anywhere = pl.BlockSpec(memory_space=pl.ANY)
    part = jax.ShapeDtypeStruct((HALF, TILE, 128), jnp.float32)
    whole = jax.ShapeDtypeStruct((2 * HALF, TILE, 128), jnp.float32)
    out_shape = [whole, part] if last else [part] * 3

    def kernel(*refs):
        step_kernel(first, last, *refs)

    return pl.pallas_call(
        kernel,
        out_shape=out_shape,
        in_specs=[anywhere] * len(operands),
        out_specs=[anywhere] * len(out_shape),
        scratch_shapes=[
            pltpu.VMEM((24, TILE, 128), jnp.float32),
            pltpu.VMEM((24, TILE, 128), jnp.float32),
            pltpu.VMEM((LISTED, TILE), jnp.int32),
            pltpu.SMEM((8, 128), jnp.int32),
            pltpu.SemaphoreType.DMA((8,)),
        ],
        compiler_params=pltpu.CompilerParams(vmem_limit_bytes=32 * 1024 * 1024),
        cost_estimate=pl.CostEstimate(
            flops=2 * 10**9, bytes_accessed=10 * 2**20, transcendentals=8 * TILE * TILE
        ),
    )(*operands)


def body(vertex, context, tile_count, tile_vert, tile_context, positives, negatives):
    groups, members = lax.axis_size("outer"), lax.axis_size("inner")
    steps = tile_count.shape[0]

    def sent(array, even, odd):
        return lax.ppermute(array, AXES, route(groups, members, even, odd))

    lists = pack(tile_count, tile_vert, tile_context, positives, negatives)
    lists = [lists[0]] + [sent(lists[s], (0, 0), (0, -s)) for s in range(1, steps)]
    state = [vertex.reshape(-1, TILE, 128), context.reshape(-1, TILE, 128)]
    for s in range(steps):
        state = train(s == 0, s == steps - 1, [*state, lists[s]])
        if s + 1 < steps:
            x, y, z = state
            state = [sent(x, (0, 1), (0, -1)), sent(y, (0, 1), (0, 0)), z]
    vertex, context = state
    vertex = sent(vertex.reshape(-1, 128), (1, 0), (1, steps - 1))
    context = sent(context.reshape(-1, 128), (0, 0), (0, steps - 1))
    return vertex, context


def solution(mesh):
    return jax.shard_map(
        body,
        mesh=mesh,
        in_specs=(
            P(AXES, None),
            P(AXES, None),
            P(AXES),
            P(AXES, None),
            P(AXES, None),
            P(AXES, None, None),
            P(AXES, None, None, None),
        ),
        out_specs=(P(AXES, None), P(AXES, None)),
        check_vma=False,
    )
```

```python
import jax
import jax.numpy as jnp
from jax import lax
from jax.experimental import pallas as pl
from jax.experimental.pallas import tpu as pltpu
from jax.sharding import PartitionSpec as P

TILE = 256
WIDTH = 128
SLOTS = 8
NEG = 4
AXES = ("outer", "inner")
META = 40
LISTED = 48
VERT_TILES = 16
CTX_TILES = 8


def route(groups, members, odd, move):
    pairs = []
    for o in range(odd, groups, 2):
        for i in range(members):
            to = ((o + move[0]) % groups) * members + (i + move[1]) % members
            pairs.append((o * members + i, to))
    return pairs


def tiles(n):
    return jax.ShapeDtypeStruct((n, TILE, WIDTH), jnp.float32)


ANY = pl.BlockSpec(memory_space=pl.ANY)
HBM = pl.BlockSpec(memory_space=pltpu.HBM)
SMEM = pl.BlockSpec(memory_space=pltpu.SMEM)
VMEM = pl.BlockSpec(memory_space=pltpu.VMEM)


def pack_kernel(count, vert, ctx, positives, negatives, after, *packed):
    lane = lax.broadcasted_iota(jnp.int32, (8, 128), 1)
    for s, out in enumerate(packed, 1):
        out[0:8, :] = positives[s]
        for t in range(SLOTS):
            out[8 + NEG * t : 8 + NEG * t + NEG, :] = negatives[s, t]
        meta = jnp.where(lane == 16, count[s], 0)
        for t in range(SLOTS):
            meta = jnp.where(lane == t, vert[s, t], meta)
            meta = jnp.where(lane == 8 + t, ctx[s, t], meta)
        out[META:LISTED, 0:128] = meta
        out[META:LISTED, 128:256] = meta


def pack(lists, after):
    steps = lists[1].shape[0]
    return pl.pallas_call(
        pack_kernel,
        out_shape=[jax.ShapeDtypeStruct((LISTED, TILE), jnp.int32)] * (steps - 1),
        in_specs=[SMEM, SMEM, SMEM, VMEM, VMEM, ANY],
        out_specs=[VMEM] * (steps - 1),
        compiler_params=pltpu.CompilerParams(vmem_limit_bytes=2 * 1024 * 1024),
    )(*lists, after)


def halves(x):
    high = x.astype(jnp.bfloat16)
    return high, (x - high.astype(jnp.float32)).astype(jnp.bfloat16)


def dot(a, b, dims):
    return lax.dot_general(a, b, (dims, ((), ())), preferred_element_type=jnp.float32)


def slot_update(v, c, pos_row, neg_rows, live):
    v_hi, v_lo = halves(v)
    c_hi, c_lo = halves(c)
    c_both = jnp.concatenate([c_hi, c_lo], axis=1)
    v_both = jnp.concatenate([v_hi, v_lo], axis=1)
    scores = dot(c_both, jnp.concatenate([v_hi, v_hi], axis=1), ((1,), (1,)))
    scores = scores + dot(c_hi, v_lo, ((1,), (1,)))
    column = lax.broadcasted_iota(jnp.int32, (TILE, TILE), 0)
    at_pos = pos_row == column
    quarter = jnp.where(live, -0.25, 0.0)
    scale = jnp.where(at_pos, quarter, 0.0)
    for row in neg_rows:
        scale = scale + jnp.where(row == column, quarter, 0.0)
    grad = scale * jnp.tanh(0.5 * scores) + (scale + jnp.where(at_pos, -2.0 * quarter, 0.0))
    g_hi, g_lo = halves(grad)
    dc = dot(g_hi, v_both, ((1,), (0,)))
    dc = dc[:, :WIDTH] + dc[:, WIDTH:] + dot(g_lo, v_hi, ((1,), (0,)))
    dv = dot(g_hi, c_both, ((0,), (0,)))
    dv = dv[:, :WIDTH] + dv[:, WIDTH:] + dot(g_lo, c_hi, ((0,), (0,)))
    return dv, dc


def step_kernel(odd, first, half, n_lists, n_after, *refs):
    n_move = CTX_TILES // 2 if odd else VERT_TILES // 2
    move_in, stay_in, *refs = refs
    total_in = None
    if half:
        total_in, *refs = refs
    list_refs, refs = refs[:n_lists], refs[n_lists:]
    move_out, stay_out, *refs = refs[n_after:]
    m_old, m_new, s_old, s_new, chosen, sems, *refs = refs

    @pl.when(lax.rem(lax.axis_index("outer"), 2) == odd)
    def work():
        source = move_in.at[pl.ds(half * n_move, n_move)] if first else move_in
        loads = [
            pltpu.make_async_copy(source, m_old, sems.at[0]),
            pltpu.make_async_copy(stay_in, s_old, sems.at[1]),
            pltpu.make_async_copy(source, m_new, sems.at[2]),
            pltpu.make_async_copy(total_in if half else stay_in, s_new, sems.at[3]),
        ]
        if first:
            count_ref, vert_ref, ctx_ref, positives, negatives = list_refs
            for load in loads:
                load.start()
            count = count_ref[0]

            def vert(t):
                return vert_ref[0, t]

            def ctx(t):
                return ctx_ref[0, t]

            def pos_row(t):
                return positives[0, pl.ds(t, 1), :]

            def neg_row(t, k):
                return negatives[0, t, pl.ds(k, 1), :]
        else:
            listed, meta = refs
            heads = pltpu.make_async_copy(
                list_refs[0].at[META:LISTED, 0:128], meta, sems.at[4]
            )
            rows = pltpu.make_async_copy(list_refs[0], listed, sems.at[5])
            heads.start()
            rows.start()
            for load in loads:
                load.start()
            heads.wait()
            count = meta[0, 16]

            def vert(t):
                return meta[0, t]

            def ctx(t):
                return meta[0, 8 + t]

            def pos_row(t):
                return listed[pl.ds(t, 1), :]

            def neg_row(t, k):
                return listed[pl.ds(8 + NEG * t + k, 1), :]

        mine = jnp.int32(0)
        for t in range(SLOTS):
            chosen[mine] = t
            moving = ctx(t) if odd else vert(t)
            here = (t < count) & (moving // n_move == half)
            mine = mine + here.astype(jnp.int32)
        if not first:
            rows.wait()
        for load in loads:
            load.wait()

        def one(t, live):
            vi, ci = vert(t), ctx(t)
            if odd:
                ci = ci - half * n_move
                ci = jnp.where(live, ci, 0)
                v, c = s_old[vi], m_old[ci]
            else:
                vi = vi - half * n_move
                vi = jnp.where(live, vi, 0)
                v, c = m_old[vi], s_old[ci]
            rows = [neg_row(t, k) for k in range(NEG)]
            return vi, ci, *slot_update(v, c, pos_row(t), rows, live)

        def pair(n, carry):
            results = []
            for at in (2 * n, 2 * n + 1):
                live = at < mine
                results.append(one(chosen[jnp.where(live, at, 0)], live))
            for vi, ci, dv, dc in results:
                if odd:
                    s_new[vi] += dv
                    m_new[ci] += dc
                else:
                    m_new[vi] += dv
                    s_new[ci] += dc
            return carry

        lax.fori_loop(0, (mine + 1) // 2, pair, 0)
        stores = [
            pltpu.make_async_copy(m_new, move_out, sems.at[0]),
            pltpu.make_async_copy(s_new, stay_out, sems.at[1]),
        ]
        for store in stores:
            store.start()
        for store in stores:
            store.wait()


def step(odd, first, half, moving, staying, total, lists, after):
    n_move = CTX_TILES // 2 if odd else VERT_TILES // 2
    n_stay = VERT_TILES if odd else CTX_TILES
    place = HBM if first else ANY
    operands = [moving, staying]
    specs = [place, place]
    if half:
        operands.append(total)
        specs.append(ANY)
    operands += lists
    if first:
        specs += [SMEM, SMEM, SMEM, VMEM, VMEM]
    else:
        specs += [ANY]
    operands += after
    specs += [ANY] * len(after)
    scratch = [
        pltpu.VMEM((n_move, TILE, WIDTH), jnp.float32),
        pltpu.VMEM((n_move, TILE, WIDTH), jnp.float32),
        pltpu.VMEM((n_stay, TILE, WIDTH), jnp.float32),
        pltpu.VMEM((n_stay, TILE, WIDTH), jnp.float32),
        pltpu.SMEM((SLOTS + 1,), jnp.int32),
        pltpu.SemaphoreType.DMA((6,)),
    ]
    if not first:
        scratch += [
            pltpu.VMEM((LISTED, TILE), jnp.int32),
            pltpu.SMEM((8, 128), jnp.int32),
        ]

    def kernel(*refs):
        step_kernel(odd, first, half, len(lists), len(after), *refs)

    return pl.pallas_call(
        kernel,
        out_shape=[tiles(n_move), tiles(n_stay)],
        in_specs=specs,
        out_specs=[ANY, ANY],
        scratch_shapes=scratch,
        compiler_params=pltpu.CompilerParams(vmem_limit_bytes=24 * 1024 * 1024),
        cost_estimate=pl.CostEstimate(
            flops=10**9, bytes_accessed=6 * 2**20, transcendentals=4 * TILE * TILE
        ),
    )(*operands)


def finish_kernel(whole, low, high, stayed, ctx_low, ctx_high, vertex, context, sems):
    odd = lax.rem(lax.axis_index("outer"), 2)

    def run(copies):
        copies = [
            pltpu.make_async_copy(source, to, sems.at[n])
            for n, (source, to) in enumerate(copies)
        ]
        for copy in copies:
            copy.start()
        for copy in copies:
            copy.wait()

    @pl.when(odd == 0)
    def even_group():
        run([(whole, vertex), (stayed, context)])

    @pl.when(odd == 1)
    def odd_group():
        half = VERT_TILES // 2
        quarter = CTX_TILES // 2
        run(
            [
                (low, vertex.at[pl.ds(0, half)]),
                (high, vertex.at[pl.ds(half, half)]),
                (ctx_low, context.at[pl.ds(0, quarter)]),
                (ctx_high, context.at[pl.ds(quarter, quarter)]),
            ]
        )


def finish(*operands):
    return pl.pallas_call(
        finish_kernel,
        out_shape=[tiles(VERT_TILES), tiles(CTX_TILES)],
        in_specs=[ANY] * 6,
        out_specs=[HBM, HBM],
        scratch_shapes=[pltpu.SemaphoreType.DMA((4,))],
        compiler_params=pltpu.CompilerParams(vmem_limit_bytes=1024 * 1024),
    )(*operands)


def body(vertex, context, *lists):
    groups, members = lax.axis_size("outer"), lax.axis_size("inner")
    steps = lists[0].shape[0]

    def sent(array, odd, move):
        return lax.ppermute(array, AXES, route(groups, members, odd, move))

    vertex = vertex.reshape(-1, TILE, WIDTH)
    context = context.reshape(-1, TILE, WIDTH)
    last = []

    def turn(odd, s, h, moving, staying, total, listed, *after):
        out, total = step(odd, s == 0, h, moving, staying, total, listed, [*last, *after])
        last[:] = [total]
        return out, total

    e = [None, None]
    o = [None, None]
    c_total = v_total = None
    for h in (0, 1):
        x, c_total = turn(0, 0, h, vertex, context, c_total, lists)
        e[h] = sent(x, 0, (0, 1))
        x, v_total = turn(1, 0, h, context, vertex, v_total, lists)
        o[h] = sent(x, 1, (0, -1))
    own = [None, *pack(lists, last[0])]
    theirs = [None] + [sent(own[s], 1, (0, -s)) for s in range(1, steps)]

    def even_pass(s):
        nonlocal c_total
        old, acc = c_total, None
        for h in (0, 1):
            after = [o[h]] if s == 2 else []
            x, acc = turn(0, s, h, e[h], old, acc, [own[s]], *after)
            e[h] = sent(x, 0, (0, 1) if s + 1 < steps else (1, 0))
        c_total = acc

    def odd_pass(s):
        nonlocal v_total
        old, acc = v_total, None
        for h in (0, 1):
            after = theirs[2:] if s == 1 and h == 0 else []
            x, acc = turn(1, s, h, o[h], old, acc, [theirs[s]], *after)
            o[h] = sent(x, 1, (0, -1) if s + 1 < steps else (0, steps - 1))
        v_total = acc

    odd_pass(1)
    even_pass(1)
    odd_pass(2)
    odd_pass(3)
    whole = sent(v_total, 1, (1, steps - 1))
    even_pass(2)
    even_pass(3)
    vertex, context = finish(whole, e[0], e[1], c_total, o[0], o[1])
    return vertex.reshape(-1, WIDTH), context.reshape(-1, WIDTH)


def solution(mesh):
    return jax.shard_map(
        body,
        mesh=mesh,
        in_specs=(
            P(AXES, None),
            P(AXES, None),
            P(AXES),
            P(AXES, None),
            P(AXES, None),
            P(AXES, None, None),
            P(AXES, None, None, None),
        ),
        out_specs=(P(AXES, None), P(AXES, None)),
        check_vma=False,
    )
```

```python
import jax
import jax.numpy as jnp
from jax import lax
from jax.experimental import pallas as pl
from jax.experimental.pallas import tpu as pltpu
from jax.sharding import PartitionSpec as P

TILE = 256
WIDTH = 128
SLOTS = 8
NEG = 4
AXES = ("outer", "inner")
META = 40
LISTED = 48
VERT_TILES = 16
CTX_TILES = 8
FIRST_LIMIT = 60 * 1024 * 1024


def route(groups, members, odd, move):
    pairs = []
    for o in range(odd, groups, 2):
        for i in range(members):
            to = ((o + move[0]) % groups) * members + (i + move[1]) % members
            pairs.append((o * members + i, to))
    return pairs


def tiles(n):
    return jax.ShapeDtypeStruct((n, TILE, WIDTH), jnp.float32)


ANY = pl.BlockSpec(memory_space=pl.ANY)
HBM = pl.BlockSpec(memory_space=pltpu.HBM)
SMEM = pl.BlockSpec(memory_space=pltpu.SMEM)
VMEM = pl.BlockSpec(memory_space=pltpu.VMEM)


def halves(x):
    high = x.astype(jnp.bfloat16)
    return high, (x - high.astype(jnp.float32)).astype(jnp.bfloat16)


def dot(a, b, dims):
    return lax.dot_general(a, b, (dims, ((), ())), preferred_element_type=jnp.float32)


def slot_update(v, c, pos_row, neg_rows, live):
    v_hi, v_lo = halves(v)
    c_hi, c_lo = halves(c)
    c_both = jnp.concatenate([c_hi, c_lo], axis=1)
    v_both = jnp.concatenate([v_hi, v_lo], axis=1)
    scores = dot(c_both, jnp.concatenate([v_hi, v_hi], axis=1), ((1,), (1,)))
    scores = scores + dot(c_hi, v_lo, ((1,), (1,)))
    column = lax.broadcasted_iota(jnp.int32, (TILE, TILE), 0)
    at_pos = pos_row == column
    quarter = jnp.where(live, -0.25, 0.0)
    scale = jnp.where(at_pos, quarter, 0.0)
    for row in neg_rows:
        scale = scale + jnp.where(row == column, quarter, 0.0)
    grad = scale * jnp.tanh(0.5 * scores) + (scale + jnp.where(at_pos, -2.0 * quarter, 0.0))
    g_hi, g_lo = halves(grad)
    dc = dot(g_hi, v_both, ((1,), (0,)))
    dc = dc[:, :WIDTH] + dc[:, WIDTH:] + dot(g_lo, v_hi, ((1,), (0,)))
    dv = dot(g_hi, c_both, ((0,), (0,)))
    dv = dv[:, :WIDTH] + dv[:, WIDTH:] + dot(g_lo, c_hi, ((0,), (0,)))
    return dv, dc


def choose(chosen, count, here):
    mine = jnp.int32(0)
    for t in range(SLOTS):
        chosen[mine] = t
        mine = mine + ((t < count) & here(t)).astype(jnp.int32)
    return mine


def run_pairs(chosen, mine, one):
    def pair(n, carry):
        results = []
        for at in (2 * n, 2 * n + 1):
            live = at < mine
            results.append(one(chosen[jnp.where(live, at, 0)], live))
        for v_to, vi, dv, c_to, ci, dc in results:
            v_to[vi] += dv
            c_to[ci] += dc
        return carry

    lax.fori_loop(0, (mine + 1) // 2, pair, 0)


def started(copies):
    for copy in copies:
        copy.start()
    return copies


def waited(copies):
    for copy in copies:
        copy.wait()


def first_kernel(
    vertex, context, count, vert, ctx, positives, negatives,
    low_out, high_out, moved_out, ctx_out, vert_out, *refs
):
    packed, refs = refs[:-6], refs[-6:]
    v_old, v_new, c_old, c_new, chosen, sems = refs
    odd = lax.rem(lax.axis_index("outer"), 2)
    half = VERT_TILES // 2
    loads = started(
        [
            pltpu.make_async_copy(context, c_old, sems.at[0]),
            pltpu.make_async_copy(vertex, v_old, sems.at[1]),
            pltpu.make_async_copy(context, c_new, sems.at[2]),
            pltpu.make_async_copy(vertex, v_new, sems.at[3]),
        ]
    )
    lane = lax.broadcasted_iota(jnp.int32, (8, 128), 1)
    for s, out in enumerate(packed, 1):
        out[0:8, :] = positives[s]
        for t in range(SLOTS):
            out[8 + NEG * t : 8 + NEG * t + NEG, :] = negatives[s, t]
        meta = jnp.where(lane == 16, count[s], 0)
        for t in range(SLOTS):
            meta = jnp.where(lane == t, vert[s, t], meta)
            meta = jnp.where(lane == 8 + t, ctx[s, t], meta)
        out[META:LISTED, 0:128] = meta
        out[META:LISTED, 128:256] = meta
    mine = choose(chosen, count[0], lambda t: True)
    waited(loads)

    def one(t, live):
        vi, ci = vert[0, t], ctx[0, t]
        rows = [negatives[0, t, pl.ds(k, 1), :] for k in range(NEG)]
        pos_row = positives[0, pl.ds(t, 1), :]
        dv, dc = slot_update(v_old[vi], c_old[ci], pos_row, rows, live)
        return v_new, vi, dv, c_new, ci, dc

    run_pairs(chosen, mine, one)

    @pl.when(odd == 0)
    def even_group():
        waited(
            started(
                [
                    pltpu.make_async_copy(v_new.at[pl.ds(0, half)], low_out, sems.at[0]),
                    pltpu.make_async_copy(v_new.at[pl.ds(half, half)], high_out, sems.at[1]),
                    pltpu.make_async_copy(c_new, ctx_out, sems.at[2]),
                ]
            )
        )

    @pl.when(odd == 1)
    def odd_group():
        waited(
            started(
                [
                    pltpu.make_async_copy(c_new, moved_out, sems.at[0]),
                    pltpu.make_async_copy(v_new, vert_out, sems.at[1]),
                ]
            )
        )


def first_step(vertex, context, lists):
    steps = lists[0].shape[0]
    half = VERT_TILES // 2
    listed = jax.ShapeDtypeStruct((LISTED, TILE), jnp.int32)
    return pl.pallas_call(
        first_kernel,
        out_shape=[tiles(half), tiles(half), tiles(CTX_TILES), tiles(CTX_TILES), tiles(VERT_TILES)]
        + [listed] * (steps - 1),
        in_specs=[ANY, ANY, SMEM, SMEM, SMEM, VMEM, VMEM],
        out_specs=[ANY] * 5 + [VMEM] * (steps - 1),
        scratch_shapes=[
            pltpu.VMEM((VERT_TILES, TILE, WIDTH), jnp.float32),
            pltpu.VMEM((VERT_TILES, TILE, WIDTH), jnp.float32),
            pltpu.VMEM((CTX_TILES, TILE, WIDTH), jnp.float32),
            pltpu.VMEM((CTX_TILES, TILE, WIDTH), jnp.float32),
            pltpu.SMEM((SLOTS + 1,), jnp.int32),
            pltpu.SemaphoreType.DMA((4,)),
        ],
        compiler_params=pltpu.CompilerParams(vmem_limit_bytes=FIRST_LIMIT),
        cost_estimate=pl.CostEstimate(flops=1000, bytes_accessed=1000, transcendentals=0),
    )(vertex, context, *lists)


def step_kernel(odd, half, joined, n_after, *refs):
    n_move = CTX_TILES if odd else VERT_TILES // 2
    move_in, stay_in, *refs = refs
    total_in = stay_in
    if joined:
        total_in, *refs = refs
    list_in, *refs = refs
    move_out, stay_out, *refs = refs[n_after:]
    m_old, m_new, s_old, s_new, listed, meta, chosen, sems = refs

    @pl.when(lax.rem(lax.axis_index("outer"), 2) == odd)
    def work():
        heads = pltpu.make_async_copy(list_in.at[META:LISTED, 0:128], meta, sems.at[4])
        heads.start()
        loads = started(
            [
                pltpu.make_async_copy(list_in, listed, sems.at[5]),
                pltpu.make_async_copy(move_in, m_old, sems.at[0]),
                pltpu.make_async_copy(stay_in, s_old, sems.at[1]),
                pltpu.make_async_copy(move_in, m_new, sems.at[2]),
                pltpu.make_async_copy(total_in, s_new, sems.at[3]),
            ]
        )
        heads.wait()

        def here(t):
            return True if odd else meta[0, t] // n_move == half

        mine = choose(chosen, meta[0, 16], here)
        waited(loads)

        def one(t, live):
            vi, ci = meta[0, t], meta[0, 8 + t]
            rows = [listed[pl.ds(8 + NEG * t + k, 1), :] for k in range(NEG)]
            pos_row = listed[pl.ds(t, 1), :]
            if odd:
                dv, dc = slot_update(s_old[vi], m_old[ci], pos_row, rows, live)
                return s_new, vi, dv, m_new, ci, dc
            vi = lax.rem(vi, n_move)
            dv, dc = slot_update(m_old[vi], s_old[ci], pos_row, rows, live)
            return m_new, vi, dv, s_new, ci, dc

        run_pairs(chosen, mine, one)
        waited(
            started(
                [
                    pltpu.make_async_copy(m_new, move_out, sems.at[0]),
                    pltpu.make_async_copy(s_new, stay_out, sems.at[1]),
                ]
            )
        )


def step(odd, half, moving, staying, total, listed, after):
    n_move = CTX_TILES if odd else VERT_TILES // 2
    n_stay = VERT_TILES if odd else CTX_TILES
    operands = [moving, staying] + ([] if total is None else [total]) + [listed, *after]

    def kernel(*refs):
        step_kernel(odd, half, total is not None, len(after), *refs)

    return pl.pallas_call(
        kernel,
        out_shape=[tiles(n_move), tiles(n_stay)],
        in_specs=[ANY] * len(operands),
        out_specs=[ANY, ANY],
        scratch_shapes=[
            pltpu.VMEM((n_move, TILE, WIDTH), jnp.float32),
            pltpu.VMEM((n_move, TILE, WIDTH), jnp.float32),
            pltpu.VMEM((n_stay, TILE, WIDTH), jnp.float32),
            pltpu.VMEM((n_stay, TILE, WIDTH), jnp.float32),
            pltpu.VMEM((LISTED, TILE), jnp.int32),
            pltpu.SMEM((8, 128), jnp.int32),
            pltpu.SMEM((SLOTS + 1,), jnp.int32),
            pltpu.SemaphoreType.DMA((6,)),
        ],
        compiler_params=pltpu.CompilerParams(vmem_limit_bytes=20 * 1024 * 1024),
        cost_estimate=pl.CostEstimate(flops=1000, bytes_accessed=1000, transcendentals=0),
    )(*operands)


def finish_kernel(whole, low, high, stayed, home, vertex, context, sems):
    odd = lax.rem(lax.axis_index("outer"), 2)

    def run(copies):
        waited(
            started(
                [
                    pltpu.make_async_copy(source, to, sems.at[n])
                    for n, (source, to) in enumerate(copies)
                ]
            )
        )

    @pl.when(odd == 0)
    def even_group():
        run([(whole, vertex), (stayed, context)])

    @pl.when(odd == 1)
    def odd_group():
        half = VERT_TILES // 2
        run(
            [
                (low, vertex.at[pl.ds(0, half)]),
                (high, vertex.at[pl.ds(half, half)]),
                (home, context),
            ]
        )


def finish(*operands):
    return pl.pallas_call(
        finish_kernel,
        out_shape=[tiles(VERT_TILES), tiles(CTX_TILES)],
        in_specs=[ANY] * 5,
        out_specs=[HBM, HBM],
        scratch_shapes=[pltpu.SemaphoreType.DMA((3,))],
        compiler_params=pltpu.CompilerParams(vmem_limit_bytes=1024 * 1024),
    )(*operands)


def body(vertex, context, *lists):
    groups, members = lax.axis_size("outer"), lax.axis_size("inner")
    steps = lists[0].shape[0]

    def sent(array, odd, move):
        return lax.ppermute(array, AXES, route(groups, members, odd, move))

    vertex = vertex.reshape(-1, TILE, WIDTH)
    context = context.reshape(-1, TILE, WIDTH)
    low, high, o, c_state, v_state, *own = first_step(vertex, context, lists)
    e = [sent(low, 0, (0, 1)), sent(high, 0, (0, 1))]
    o = sent(o, 1, (0, -1))
    theirs = [sent(own[s - 1], 1, (0, -s)) for s in range(1, steps)]
    last = []

    def even_half(s, h, total, *after):
        x, total = step(0, h, e[h], c_state, total, own[s - 1], [*last, *after])
        last[:] = [total]
        e[h] = sent(x, 0, (0, 1) if s + 1 < steps else (1, 0))
        return total

    def odd_pass(s):
        nonlocal o, v_state
        x, v_state = step(1, 0, o, v_state, None, theirs[s - 1], last)
        last[:] = [v_state]
        o = sent(x, 1, (0, -1) if s + 1 < steps else (0, steps - 1))

    odd_pass(1)
    total = even_half(1, 0, None)
    odd_pass(2)
    c_state = even_half(1, 1, total)
    odd_pass(3)
    whole = sent(v_state, 1, (1, steps - 1))
    c_state = even_half(2, 1, even_half(2, 0, None))
    c_state = even_half(3, 1, even_half(3, 0, None, o))
    vertex, context = finish(whole, *e, c_state, o)
    return vertex.reshape(-1, WIDTH), context.reshape(-1, WIDTH)


def solution(mesh):
    return jax.shard_map(
        body,
        mesh=mesh,
        in_specs=(
            P(AXES, None),
            P(AXES, None),
            P(AXES),
            P(AXES, None),
            P(AXES, None),
            P(AXES, None, None),
            P(AXES, None, None, None),
        ),
        out_specs=(P(AXES, None), P(AXES, None)),
        check_vma=False,
    )
```

```python
import jax
import jax.numpy as jnp
from jax import lax
from jax.experimental import pallas as pl
from jax.experimental.pallas import tpu as pltpu
from jax.sharding import PartitionSpec as P

TILE = 256
WIDTH = 128
SLOTS = 8
NEG = 4
AXES = ("outer", "inner")
META = 40
SIDE = 48
LISTED = 96
VERT_TILES = 16
CTX_TILES = 8
HALF = 8 * TILE
FIRST_LIMIT = 60 * 1024 * 1024
STEP_LIMIT = 20 * 1024 * 1024

ANY = pl.BlockSpec(memory_space=pl.ANY)
HBM = pl.BlockSpec(memory_space=pltpu.HBM)


def route(groups, members, odd, move):
    pairs = []
    for o in range(odd, groups, 2):
        for i in range(members):
            to = ((o + move[0]) % groups) * members + (i + move[1]) % members
            pairs.append((o * members + i, to))
    return pairs


def wide(rows):
    return jax.ShapeDtypeStruct((rows, WIDTH), jnp.float32)


def vmem(rows):
    return pltpu.VMEM((rows, WIDTH), jnp.float32)


def tile(n):
    return pl.ds(pl.multiple_of(n * TILE, TILE), TILE)


def started(copies):
    for copy in copies:
        copy.start()
    return copies


def waited(copies):
    for copy in copies:
        copy.wait()


def moved(pairs, sems, first=0):
    return started(
        [
            pltpu.make_async_copy(source, to, sems.at[first + n])
            for n, (source, to) in enumerate(pairs)
        ]
    )


def halves(x):
    high = x.astype(jnp.bfloat16)
    return high, (x - high.astype(jnp.float32)).astype(jnp.bfloat16)


def dot(a, b, dims):
    return lax.dot_general(a, b, (dims, ((), ())), preferred_element_type=jnp.float32)


def slot_update(v, c, pos_row, neg_rows, live):
    v_hi, v_lo = halves(v)
    c_hi, c_lo = halves(c)
    c_both = jnp.concatenate([c_hi, c_lo], axis=1)
    v_both = jnp.concatenate([v_hi, v_lo], axis=1)
    scores = dot(
        jnp.concatenate([c_hi, c_lo, c_hi], axis=1),
        jnp.concatenate([v_hi, v_hi, v_lo], axis=1),
        ((1,), (1,)),
    )
    column = lax.broadcasted_iota(jnp.int32, (TILE, TILE), 0)
    at_pos = pos_row == column
    quarter = jnp.where(live, -0.25, 0.0)
    scale = jnp.where(at_pos, quarter, 0.0)
    for row in neg_rows:
        scale = scale + jnp.where(row == column, quarter, 0.0)
    grad = scale * jnp.tanh(0.5 * scores) + (scale + jnp.where(at_pos, -2.0 * quarter, 0.0))
    g_hi, g_lo = halves(grad)
    dc = dot(
        jnp.concatenate([g_hi, g_lo], axis=1),
        jnp.concatenate([v_both, v_both], axis=0),
        ((1,), (0,)),
    )
    dv = dot(
        jnp.concatenate([g_hi, g_lo], axis=0),
        jnp.concatenate([c_both, c_both], axis=0),
        ((0,), (0,)),
    )
    return dv[:, :WIDTH] + dv[:, WIDTH:], dc[:, :WIDTH] + dc[:, WIDTH:]


def choose(chosen, count, here):
    mine = jnp.int32(0)
    for t in range(SLOTS):
        chosen[mine] = t
        mine = mine + ((t < count) & here(t)).astype(jnp.int32)
    return mine


def run_pairs(chosen, mine, one):
    def pair(n, carry):
        results = []
        for at in (2 * n, 2 * n + 1):
            live = at < mine
            results.append(one(chosen[jnp.where(live, at, 0)], live))
        for v_to, vi, dv, c_to, ci, dc in results:
            v_to[tile(vi), :] += dv
            c_to[tile(ci), :] += dc
        return carry

    lax.fori_loop(0, (mine + 1) // 2, pair, 0)


def group_odd():
    return lax.rem(lax.axis_index("outer"), 2)


def first_kernel(steps, *refs):
    vertex, context, count_in, vert_in, ctx_in, pos_in, neg_in, *refs = refs
    low_out, high_out, moved_out, ctx_out, vert_out, own_out, names_out, *refs = refs
    v_old, v_new, c_old, c_new, count, vert, ctx, pos, neg, own, chosen, sems = refs
    heads = moved([(count_in, count), (vert_in, vert), (ctx_in, ctx)], sems)
    lists = moved([(pos_in, pos), (neg_in, neg)], sems, 3)
    loads = moved([(context, c_old), (vertex, v_old)], sems, 5)
    waited(heads)
    mine = choose(chosen, count[0], lambda t: True)
    waited(lists)
    lane = lax.broadcasted_iota(jnp.int32, (8, 128), 1)
    for s in range(1, steps):
        base = LISTED * (s - 1)
        for side in (0, 1):
            lanes = slice(128 * side, 128 * side + 128)
            at = base + SIDE * side
            own[at : at + 8, :] = pos[s, :, lanes].astype(jnp.float32)
            for t in range(SLOTS):
                rows = slice(at + 8 + NEG * t, at + 8 + NEG * t + NEG)
                own[rows, :] = neg[s, t, :, lanes].astype(jnp.float32)
        meta = jnp.where(lane == 16, count[s], 0)
        for t in range(SLOTS):
            meta = jnp.where(lane == t, vert[s, t], meta)
            meta = jnp.where(lane == 8 + t, ctx[s, t], meta)
        meta = meta.astype(jnp.float32)
        own[base + META : base + SIDE, :] = meta
        own[base + SIDE + META : base + LISTED, :] = meta
    waited(loads)

    def fill(n, carry):
        c_new[tile(n), :] = c_old[tile(n), :]
        v_new[tile(2 * n), :] = v_old[tile(2 * n), :]
        v_new[tile(2 * n + 1), :] = v_old[tile(2 * n + 1), :]
        return carry

    lax.fori_loop(0, CTX_TILES, fill, 0)

    def one(t, live):
        vi, ci = vert[0, t], ctx[0, t]
        rows = [neg[0, t, pl.ds(k, 1), :] for k in range(NEG)]
        pos_row = pos[0, pl.ds(t, 1), :]
        dv, dc = slot_update(v_old[tile(vi), :], c_old[tile(ci), :], pos_row, rows, live)
        return v_new, vi, dv, c_new, ci, dc

    run_pairs(chosen, mine, one)
    odd = group_odd()

    @pl.when(odd == 0)
    def even_group():
        stores = [
            (v_new.at[pl.ds(0, HALF)], low_out),
            (v_new.at[pl.ds(HALF, HALF)], high_out),
            (c_new, ctx_out),
            (own, own_out),
        ]
        waited(moved(stores, sems))

    @pl.when(odd == 1)
    def odd_group():
        stores = [
            (c_new, moved_out.at[pl.ds(0, HALF)]),
            (own, moved_out.at[pl.ds(HALF, LISTED * (steps - 1))]),
            (v_new, vert_out),
            (own.at[pl.ds(LISTED * (steps - 2) + META, 8)], names_out),
        ]
        waited(moved(stores, sems))


def first_step(vertex, context, lists):
    steps = lists[0].shape[0]
    listed = LISTED * (steps - 1)

    def kernel(*refs):
        first_kernel(steps, *refs)

    return pl.pallas_call(
        kernel,
        out_shape=[
            wide(HALF),
            wide(HALF),
            wide(HALF + listed),
            wide(HALF),
            wide(2 * HALF),
            wide(listed),
            wide(8),
        ],
        in_specs=[ANY] * 7,
        out_specs=[ANY] * 7,
        scratch_shapes=[
            vmem(2 * HALF),
            vmem(2 * HALF),
            vmem(HALF),
            vmem(HALF),
            pltpu.SMEM((steps,), jnp.int32),
            pltpu.SMEM((steps, SLOTS), jnp.int32),
            pltpu.SMEM((steps, SLOTS), jnp.int32),
            pltpu.VMEM((steps, SLOTS, TILE), jnp.int32),
            pltpu.VMEM((steps, SLOTS, NEG, TILE), jnp.int32),
            vmem(listed),
            pltpu.SMEM((SLOTS + 1,), jnp.int32),
            pltpu.SemaphoreType.DMA((7,)),
        ],
        compiler_params=pltpu.CompilerParams(vmem_limit_bytes=FIRST_LIMIT),
        cost_estimate=pl.CostEstimate(flops=1000, bytes_accessed=1000, transcendentals=0),
    )(vertex, context, *lists)


def head(meta, lane):
    return meta[0, lane].astype(jnp.int32)


def listed_rows(listed, t):
    def row(r):
        both = [listed[pl.ds(r, 1), :], listed[pl.ds(SIDE + r, 1), :]]
        return jnp.concatenate(both, axis=1).astype(jnp.int32)

    return row(t), [row(8 + NEG * t + k) for k in range(NEG)]


def even_kernel(s, half, joined, n_after, *refs):
    move_in, stay_in, *refs = refs
    total_in = stay_in
    if joined:
        total_in, *refs = refs
    own, *refs = refs
    move_out, stay_out, *refs = refs[n_after:]
    m_old, m_new, s_old, s_new, listed, meta, chosen, sems = refs

    @pl.when(group_odd() == 0)
    def work():
        list_in = own.at[pl.ds(LISTED * (s - 1), LISTED)]
        heads = moved([(list_in.at[pl.ds(META, 8)], meta)], sems)
        loads = [
            (list_in, listed),
            (move_in, m_old),
            (stay_in, s_old),
            (move_in, m_new),
            (total_in, s_new),
        ]
        loads = moved(loads, sems, 1)
        waited(heads)
        mine = choose(chosen, head(meta, 16), lambda t: head(meta, t) // 8 == half)
        waited(loads)

        def one(t, live):
            vi, ci = lax.rem(head(meta, t), 8), head(meta, 8 + t)
            rows = listed_rows(listed, t)
            dv, dc = slot_update(m_old[tile(vi), :], s_old[tile(ci), :], *rows, live)
            return m_new, vi, dv, s_new, ci, dc

        run_pairs(chosen, mine, one)
        waited(moved([(m_new, move_out), (s_new, stay_out)], sems))


def even_step(s, half, moving, staying, total, own, after):
    operands = [moving, staying] + ([] if total is None else [total]) + [own, *after]

    def kernel(*refs):
        even_kernel(s, half, total is not None, len(after), *refs)

    return pl.pallas_call(
        kernel,
        out_shape=[wide(HALF), wide(HALF)],
        in_specs=[ANY] * len(operands),
        out_specs=[ANY, ANY],
        scratch_shapes=[
            vmem(HALF),
            vmem(HALF),
            vmem(HALF),
            vmem(HALF),
            vmem(LISTED),
            pltpu.SMEM((8, 128), jnp.float32),
            pltpu.SMEM((SLOTS + 1,), jnp.int32),
            pltpu.SemaphoreType.DMA((6,)),
        ],
        compiler_params=pltpu.CompilerParams(vmem_limit_bytes=STEP_LIMIT),
        cost_estimate=pl.CostEstimate(flops=1000, bytes_accessed=1000, transcendentals=0),
    )(*operands)


def part_tiles(meta, used, order):
    for n in range(VERT_TILES):
        used[n] = 0
    for t in range(SLOTS):
        at = head(meta, t)
        used[at] = jnp.where(t < head(meta, 16), 1, used[at])
    early, late = jnp.int32(0), jnp.int32(SLOTS)
    for n in range(VERT_TILES):
        soon = (used[n] == 0) & (early < SLOTS)
        order[jnp.where(soon, early, late)] = n
        early = early + soon.astype(jnp.int32)
        late = late + 1 - soon.astype(jnp.int32)


def odd_kernel(left, n_after, *refs):
    move_in, stay_in, *refs = refs
    if left == 1:
        names, *refs = refs
    refs = refs[n_after:]
    move_out, *refs = refs
    if left:
        stay_out, *refs = refs
    if left < 2:
        part_out, *refs = refs
    m_old, m_new, s_old, s_new, listed, metas, chosen, used, order, places, sems = refs

    @pl.when(group_odd() == 1)
    def work():
        meta = metas.at[0]
        split = metas.at[1 if left else 0]
        heads = [(move_in.at[pl.ds(HALF + META, 8)], meta)]
        if left == 1:
            heads.append((names, split))
        heads = moved(heads, sems)
        loads = [
            (move_in.at[pl.ds(HALF, LISTED)], listed),
            (move_in.at[pl.ds(0, HALF)], m_old),
            (stay_in, s_old),
            (move_in.at[pl.ds(0, HALF)], m_new),
            (stay_in, s_new),
        ]
        if left:
            rest = pl.ds(HALF, LISTED * left)
            loads.append((move_in.at[pl.ds(HALF + LISTED, LISTED * left)], move_out.at[rest]))
        loads = moved(loads, sems, 2)
        waited(heads)
        mine = choose(chosen, head(meta, 16), lambda t: True)
        if left < 2:
            part_tiles(split, used, order)
        waited(loads)

        def one(t, live):
            vi, ci = head(meta, t), head(meta, 8 + t)
            rows = listed_rows(listed, t)
            dv, dc = slot_update(s_old[tile(vi), :], m_old[tile(ci), :], *rows, live)
            return s_new, vi, dv, m_new, ci, dc

        run_pairs(chosen, mine, one)
        stores = [(m_new, move_out.at[pl.ds(0, HALF)])]
        if left:
            stores.append((s_new, stay_out))
        if left < 2:
            first = 0 if left else SLOTS
            stores += [
                (s_new.at[tile(order[first + n])], part_out.at[pl.ds(n * TILE, TILE)])
                for n in range(SLOTS)
            ]
        if not left:
            lane = lax.broadcasted_iota(jnp.int32, (8, 128), 1)
            spot = jnp.zeros((8, 128), jnp.int32)
            for n in range(VERT_TILES):
                spot = jnp.where(lane == n, order[n], spot)
            places[...] = spot.astype(jnp.float32)
            stores.append((places, part_out.at[pl.ds(HALF, 8)]))
        waited(moved(stores, sems))


def odd_step(left, moving, staying, names, after):
    operands = [moving, staying] + ([names] if left == 1 else [])
    out_shape = [wide(HALF + LISTED * left)]
    if left:
        out_shape.append(wide(2 * HALF))
    if left < 2:
        out_shape.append(wide(HALF if left else HALF + 8))

    def kernel(*refs):
        odd_kernel(left, len(after), *refs)

    return pl.pallas_call(
        kernel,
        out_shape=out_shape,
        in_specs=[ANY] * (len(operands) + len(after)),
        out_specs=[ANY] * len(out_shape),
        scratch_shapes=[
            vmem(HALF),
            vmem(HALF),
            vmem(2 * HALF),
            vmem(2 * HALF),
            vmem(LISTED),
            pltpu.SMEM((2, 8, 128), jnp.float32),
            pltpu.SMEM((SLOTS + 1,), jnp.int32),
            pltpu.SMEM((VERT_TILES,), jnp.int32),
            pltpu.SMEM((VERT_TILES,), jnp.int32),
            vmem(8),
            pltpu.SemaphoreType.DMA((12,)),
        ],
        compiler_params=pltpu.CompilerParams(vmem_limit_bytes=STEP_LIMIT),
        cost_estimate=pl.CostEstimate(flops=1000, bytes_accessed=1000, transcendentals=0),
    )(*operands, *after)


def finish_kernel(early, late, low, high, stayed, home, vertex, context, spots, sems):
    odd = group_odd()

    @pl.when(odd == 0)
    def even_group():
        pltpu.make_async_copy(late.at[pl.ds(HALF, 8)], spots, sems.at[0]).start()
        kept = moved([(stayed, context)], sems, 1)
        pltpu.make_async_copy(late.at[pl.ds(HALF, 8)], spots, sems.at[0]).wait()
        copies = []
        for n in range(VERT_TILES):
            source = early if n < SLOTS else late
            rows = pl.ds(n % SLOTS * TILE, TILE)
            copies.append((source.at[rows], vertex.at[tile(head(spots, n))]))
        waited(moved(copies, sems, 2))
        waited(kept)

    @pl.when(odd == 1)
    def odd_group():
        copies = [
            (low, vertex.at[pl.ds(0, HALF)]),
            (high, vertex.at[pl.ds(HALF, HALF)]),
            (home, context),
        ]
        waited(moved(copies, sems))


def finish(*operands):
    return pl.pallas_call(
        finish_kernel,
        out_shape=[wide(2 * HALF), wide(HALF)],
        in_specs=[ANY] * 6,
        out_specs=[HBM, HBM],
        scratch_shapes=[
            pltpu.SMEM((8, 128), jnp.float32),
            pltpu.SemaphoreType.DMA((2 + VERT_TILES,)),
        ],
        compiler_params=pltpu.CompilerParams(vmem_limit_bytes=1024 * 1024),
    )(*operands)


def body(vertex, context, *lists):
    groups, members = lax.axis_size("outer"), lax.axis_size("inner")
    steps = lists[0].shape[0]

    def sent(array, odd, move):
        return lax.ppermute(array, AXES, route(groups, members, odd, move))

    low, high, o, c_state, v_state, own, names = first_step(vertex, context, lists)
    names = sent(names, 1, (0, 1 - steps))
    e = [sent(low, 0, (0, 1)), sent(high, 0, (0, 1))]
    o = sent(o, 1, (0, -1))

    def even_half(s, h, total, *after):
        x, total = even_step(s, h, e[h], c_state, total, own, after)
        e[h] = sent(x, 0, (0, 1) if s + 1 < steps else (1, 0))
        return total

    def odd_whole(s):
        x, *rest = odd_step(steps - 1 - s, o, v_state, names, [])
        return sent(x, 1, (0, -1) if s + 1 < steps else (0, steps - 1)), *rest

    home = (1, steps - 1)
    total = even_half(1, 0, None)
    c_state = even_half(1, 1, total)
    total = even_half(2, 0, None)
    c_state = even_half(2, 1, total)
    o, v_state = odd_whole(1)
    o, v_state, early = odd_whole(2)
    early = sent(early, 1, home)
    o, late = odd_whole(3)
    total = even_half(3, 0, None, early, late)
    late = sent(late, 1, home)
    c_state = even_half(3, 1, total, o)
    return tuple(finish(early, late, *e, c_state, o))


def solution(mesh):
    return jax.shard_map(
        body,
        mesh=mesh,
        in_specs=(
            P(AXES, None),
            P(AXES, None),
            P(AXES),
            P(AXES, None),
            P(AXES, None),
            P(AXES, None, None),
            P(AXES, None, None, None),
        ),
        out_specs=(P(AXES, None), P(AXES, None)),
        check_vma=False,
    )
```

```python
import jax
import jax.numpy as jnp
from jax import lax
from jax.experimental import pallas as pl
from jax.experimental.pallas import tpu as pltpu
from jax.sharding import PartitionSpec as P

TILE = 256
WIDTH = 128
SLOTS = 8
NEG = 4
AXES = ("outer", "inner")
META = 40
SIDE = 48
LISTED = 96
VERT_TILES = 16
CTX_TILES = 8
HALF = 8 * TILE
FIRST_LIMIT = 60 * 1024 * 1024
STEP_LIMIT = 20 * 1024 * 1024

ANY = pl.BlockSpec(memory_space=pl.ANY)
HBM = pl.BlockSpec(memory_space=pltpu.HBM)


def route(groups, members, odd, move):
    pairs = []
    for o in range(odd, groups, 2):
        for i in range(members):
            to = ((o + move[0]) % groups) * members + (i + move[1]) % members
            pairs.append((o * members + i, to))
    return pairs


def wide(rows):
    return jax.ShapeDtypeStruct((rows, WIDTH), jnp.float32)


def vmem(rows):
    return pltpu.VMEM((rows, WIDTH), jnp.float32)


def tile(n):
    return pl.ds(pl.multiple_of(n * TILE, TILE), TILE)


def started(copies):
    for copy in copies:
        copy.start()
    return copies


def waited(copies):
    for copy in copies:
        copy.wait()


def moved(pairs, sems, first=0):
    return started(
        [
            pltpu.make_async_copy(source, to, sems.at[first + n])
            for n, (source, to) in enumerate(pairs)
        ]
    )


def halves(x):
    high = x.astype(jnp.bfloat16)
    return high, (x - high.astype(jnp.float32)).astype(jnp.bfloat16)


def dot(a, b, dims):
    return lax.dot_general(a, b, (dims, ((), ())), preferred_element_type=jnp.float32)


def slot_update(v, c, pos_row, neg_rows, live):
    v_hi, v_lo = halves(v)
    c_hi, c_lo = halves(c)
    c_both = jnp.concatenate([c_hi, c_lo], axis=1)
    v_both = jnp.concatenate([v_hi, v_lo], axis=1)
    scores = dot(
        jnp.concatenate([c_hi, c_lo, c_hi], axis=1),
        jnp.concatenate([v_hi, v_hi, v_lo], axis=1),
        ((1,), (1,)),
    )
    column = lax.broadcasted_iota(jnp.int32, (TILE, TILE), 0)
    at_pos = pos_row == column
    quarter = jnp.where(live, -0.25, 0.0)
    scale = jnp.where(at_pos, quarter, 0.0)
    for row in neg_rows:
        scale = scale + jnp.where(row == column, quarter, 0.0)
    grad = scale * jnp.tanh(0.5 * scores) + (scale + jnp.where(at_pos, -2.0 * quarter, 0.0))
    g_hi, g_lo = halves(grad)
    dc = dot(
        jnp.concatenate([g_hi, g_lo], axis=1),
        jnp.concatenate([v_both, v_both], axis=0),
        ((1,), (0,)),
    )
    dv = dot(
        jnp.concatenate([g_hi, g_lo], axis=0),
        jnp.concatenate([c_both, c_both], axis=0),
        ((0,), (0,)),
    )
    return dv[:, :WIDTH] + dv[:, WIDTH:], dc[:, :WIDTH] + dc[:, WIDTH:]


def choose(chosen, count, here):
    mine = jnp.int32(0)
    for t in range(SLOTS):
        chosen[mine] = t
        mine = mine + ((t < count) & here(t)).astype(jnp.int32)
    return mine


def run_pairs(chosen, mine, one):
    def pair(n, carry):
        results = []
        for at in (2 * n, 2 * n + 1):
            live = at < mine
            results.append(one(chosen[jnp.where(live, at, 0)], live))
        for v_to, vi, dv, c_to, ci, dc in results:
            v_to[tile(vi), :] += dv
            c_to[tile(ci), :] += dc
        return carry

    lax.fori_loop(0, (mine + 1) // 2, pair, 0)


def group_odd():
    return lax.rem(lax.axis_index("outer"), 2)


def first_kernel(steps, *refs):
    vertex, context, count_in, vert_in, ctx_in, pos_in, neg_in, *refs = refs
    low_out, high_out, moved_out, ctx_out, vert_out, own_out, names_out, *refs = refs
    v_old, v_new, c_old, c_new, count, vert, ctx, pos, neg, own, chosen, sems = refs
    heads = moved([(count_in, count), (vert_in, vert), (ctx_in, ctx)], sems)
    lists = moved([(pos_in, pos), (neg_in, neg)], sems, 3)
    loads = moved([(context, c_old), (vertex, v_old)], sems, 5)
    waited(heads)
    mine = choose(chosen, count[0], lambda t: True)
    waited(lists)
    lane = lax.broadcasted_iota(jnp.int32, (8, 128), 1)
    for s in range(1, steps):
        base = LISTED * (s - 1)
        for side in (0, 1):
            lanes = slice(128 * side, 128 * side + 128)
            at = base + SIDE * side
            own[at : at + 8, :] = pos[s, :, lanes].astype(jnp.float32)
            for t in range(SLOTS):
                rows = slice(at + 8 + NEG * t, at + 8 + NEG * t + NEG)
                own[rows, :] = neg[s, t, :, lanes].astype(jnp.float32)
        meta = jnp.where(lane == 16, count[s], 0)
        for t in range(SLOTS):
            meta = jnp.where(lane == t, vert[s, t], meta)
            meta = jnp.where(lane == 8 + t, ctx[s, t], meta)
        meta = meta.astype(jnp.float32)
        own[base + META : base + SIDE, :] = meta
        own[base + SIDE + META : base + LISTED, :] = meta
    waited(loads)

    def fill(n, carry):
        c_new[tile(n), :] = c_old[tile(n), :]
        v_new[tile(2 * n), :] = v_old[tile(2 * n), :]
        v_new[tile(2 * n + 1), :] = v_old[tile(2 * n + 1), :]
        return carry

    lax.fori_loop(0, CTX_TILES, fill, 0)

    def one(t, live):
        vi, ci = vert[0, t], ctx[0, t]
        rows = [neg[0, t, pl.ds(k, 1), :] for k in range(NEG)]
        pos_row = pos[0, pl.ds(t, 1), :]
        dv, dc = slot_update(v_old[tile(vi), :], c_old[tile(ci), :], pos_row, rows, live)
        return v_new, vi, dv, c_new, ci, dc

    run_pairs(chosen, mine, one)
    odd = group_odd()

    @pl.when(odd == 0)
    def even_group():
        stores = [
            (v_new.at[pl.ds(0, HALF)], low_out),
            (v_new.at[pl.ds(HALF, HALF)], high_out),
            (c_new, ctx_out),
            (own, own_out),
        ]
        waited(moved(stores, sems))

    @pl.when(odd == 1)
    def odd_group():
        stores = [
            (c_new, moved_out.at[pl.ds(0, HALF)]),
            (own, moved_out.at[pl.ds(HALF, LISTED * (steps - 1))]),
            (v_new, vert_out),
            (own.at[pl.ds(LISTED * (steps - 2) + META, 8)], names_out),
        ]
        waited(moved(stores, sems))


def first_step(vertex, context, lists):
    steps = lists[0].shape[0]
    listed = LISTED * (steps - 1)

    def kernel(*refs):
        first_kernel(steps, *refs)

    return pl.pallas_call(
        kernel,
        out_shape=[
            wide(HALF),
            wide(HALF),
            wide(HALF + listed),
            wide(HALF),
            wide(2 * HALF),
            wide(listed),
            wide(8),
        ],
        in_specs=[ANY] * 7,
        out_specs=[ANY] * 7,
        scratch_shapes=[
            vmem(2 * HALF),
            vmem(2 * HALF),
            vmem(HALF),
            vmem(HALF),
            pltpu.SMEM((steps,), jnp.int32),
            pltpu.SMEM((steps, SLOTS), jnp.int32),
            pltpu.SMEM((steps, SLOTS), jnp.int32),
            pltpu.VMEM((steps, SLOTS, TILE), jnp.int32),
            pltpu.VMEM((steps, SLOTS, NEG, TILE), jnp.int32),
            vmem(listed),
            pltpu.SMEM((SLOTS + 1,), jnp.int32),
            pltpu.SemaphoreType.DMA((7,)),
        ],
        compiler_params=pltpu.CompilerParams(vmem_limit_bytes=FIRST_LIMIT),
        cost_estimate=pl.CostEstimate(flops=1000, bytes_accessed=1000, transcendentals=0),
    )(vertex, context, *lists)


def head(meta, lane):
    return meta[0, lane].astype(jnp.int32)


def listed_rows(listed, t):
    def row(r):
        both = [listed[pl.ds(r, 1), :], listed[pl.ds(SIDE + r, 1), :]]
        return jnp.concatenate(both, axis=1).astype(jnp.int32)

    return row(t), [row(8 + NEG * t + k) for k in range(NEG)]


def even_kernel(s, half, joined, swaps, n_after, *refs):
    move_in, stay_in, *refs = refs
    total_in = stay_in
    if joined:
        total_in, *refs = refs
    own, *refs = refs
    if swaps:
        give, *refs = refs
    move_out, stay_out, *refs = refs[n_after:]
    m_old, m_new, s_old, s_new, listed, meta, chosen, sems = refs
    if swaps:

        @pl.when(group_odd() == 1)
        def hand_on():
            waited(moved([(give, move_out)], sems))

    @pl.when(group_odd() == 0)
    def work():
        list_in = own.at[pl.ds(LISTED * (s - 1), LISTED)]
        heads = moved([(list_in.at[pl.ds(META, 8)], meta)], sems)
        loads = [
            (list_in, listed),
            (move_in, m_old),
            (stay_in, s_old),
            (move_in, m_new),
            (total_in, s_new),
        ]
        loads = moved(loads, sems, 1)
        waited(heads)
        mine = choose(chosen, head(meta, 16), lambda t: head(meta, t) // 8 == half)
        waited(loads)

        def one(t, live):
            vi, ci = lax.rem(head(meta, t), 8), head(meta, 8 + t)
            rows = listed_rows(listed, t)
            dv, dc = slot_update(m_old[tile(vi), :], s_old[tile(ci), :], *rows, live)
            return m_new, vi, dv, s_new, ci, dc

        run_pairs(chosen, mine, one)
        stores = [(m_new, move_out.at[pl.ds(0, HALF)]), (s_new, stay_out)]
        waited(moved(stores, sems))


def even_step(s, half, moving, staying, total, own, give, after):
    swaps = give is not None
    operands = [moving, staying] + ([] if total is None else [total]) + [own]
    operands += ([give] if swaps else []) + [*after]
    size = give.shape[0] if swaps else HALF

    def kernel(*refs):
        even_kernel(s, half, total is not None, swaps, len(after), *refs)

    return pl.pallas_call(
        kernel,
        out_shape=[wide(size), wide(HALF)],
        in_specs=[ANY] * len(operands),
        out_specs=[ANY, ANY],
        scratch_shapes=[
            vmem(HALF),
            vmem(HALF),
            vmem(HALF),
            vmem(HALF),
            vmem(LISTED),
            pltpu.SMEM((8, 128), jnp.float32),
            pltpu.SMEM((SLOTS + 1,), jnp.int32),
            pltpu.SemaphoreType.DMA((6,)),
        ],
        compiler_params=pltpu.CompilerParams(vmem_limit_bytes=STEP_LIMIT),
        cost_estimate=pl.CostEstimate(flops=1000, bytes_accessed=1000, transcendentals=0),
    )(*operands)


def part_tiles(meta, used, order):
    for n in range(VERT_TILES):
        used[n] = 0
    for t in range(SLOTS):
        at = head(meta, t)
        used[at] = jnp.where(t < head(meta, 16), 1, used[at])
    early, late = jnp.int32(0), jnp.int32(SLOTS)
    for n in range(VERT_TILES):
        soon = (used[n] == 0) & (early < SLOTS)
        order[jnp.where(soon, early, late)] = n
        early = early + soon.astype(jnp.int32)
        late = late + 1 - soon.astype(jnp.int32)


def odd_kernel(left, n_after, *refs):
    move_in, stay_in, *refs = refs
    if left == 1:
        names, *refs = refs
    refs = refs[n_after:]
    move_out, *refs = refs
    if left:
        stay_out, *refs = refs
    if left < 2:
        part_out, *refs = refs
    m_old, m_new, s_old, s_new, listed, metas, chosen, used, order, places, sems = refs

    @pl.when(group_odd() == 1)
    def work():
        meta = metas.at[0]
        split = metas.at[1 if left else 0]
        heads = [(move_in.at[pl.ds(HALF + META, 8)], meta)]
        if left == 1:
            heads.append((names, split))
        heads = moved(heads, sems)
        loads = [
            (move_in.at[pl.ds(HALF, LISTED)], listed),
            (move_in.at[pl.ds(0, HALF)], m_old),
            (stay_in, s_old),
            (move_in.at[pl.ds(0, HALF)], m_new),
            (stay_in, s_new),
        ]
        if left:
            rest = pl.ds(HALF, LISTED * left)
            loads.append((move_in.at[pl.ds(HALF + LISTED, LISTED * left)], move_out.at[rest]))
        loads = moved(loads, sems, 2)
        waited(heads)
        mine = choose(chosen, head(meta, 16), lambda t: True)
        if left < 2:
            part_tiles(split, used, order)
        waited(loads)

        def one(t, live):
            vi, ci = head(meta, t), head(meta, 8 + t)
            rows = listed_rows(listed, t)
            dv, dc = slot_update(s_old[tile(vi), :], m_old[tile(ci), :], *rows, live)
            return s_new, vi, dv, m_new, ci, dc

        run_pairs(chosen, mine, one)
        stores = [(m_new, move_out.at[pl.ds(0, HALF)])]
        if left:
            stores.append((s_new, stay_out))
        if left < 2:
            first = 0 if left else SLOTS
            stores += [
                (s_new.at[tile(order[first + n])], part_out.at[pl.ds(n * TILE, TILE)])
                for n in range(SLOTS)
            ]
        if not left:
            lane = lax.broadcasted_iota(jnp.int32, (8, 128), 1)
            spot = jnp.zeros((8, 128), jnp.int32)
            for n in range(VERT_TILES):
                spot = jnp.where(lane == n, order[n], spot)
            places[...] = spot.astype(jnp.float32)
            stores.append((places, part_out.at[pl.ds(HALF, 8)]))
        waited(moved(stores, sems))


def odd_step(left, moving, staying, names, after):
    operands = [moving, staying] + ([names] if left == 1 else [])
    out_shape = [wide(HALF + LISTED * left)]
    if left:
        out_shape.append(wide(2 * HALF))
    if left < 2:
        out_shape.append(wide(HALF if left else HALF + 8))

    def kernel(*refs):
        odd_kernel(left, len(after), *refs)

    return pl.pallas_call(
        kernel,
        out_shape=out_shape,
        in_specs=[ANY] * (len(operands) + len(after)),
        out_specs=[ANY] * len(out_shape),
        scratch_shapes=[
            vmem(HALF),
            vmem(HALF),
            vmem(2 * HALF),
            vmem(2 * HALF),
            vmem(LISTED),
            pltpu.SMEM((2, 8, 128), jnp.float32),
            pltpu.SMEM((SLOTS + 1,), jnp.int32),
            pltpu.SMEM((VERT_TILES,), jnp.int32),
            pltpu.SMEM((VERT_TILES,), jnp.int32),
            vmem(8),
            pltpu.SemaphoreType.DMA((12,)),
        ],
        compiler_params=pltpu.CompilerParams(vmem_limit_bytes=STEP_LIMIT),
        cost_estimate=pl.CostEstimate(flops=1000, bytes_accessed=1000, transcendentals=0),
    )(*operands, *after)


def finish_kernel(first, second, late, stayed, home, vertex, context, spots, sems):
    odd = group_odd()

    @pl.when(odd == 0)
    def even_group():
        heads = moved([(late.at[pl.ds(HALF, 8)], spots)], sems)
        kept = moved([(stayed, context)], sems, 1)
        waited(heads)
        copies = []
        for n in range(VERT_TILES):
            source = first if n < SLOTS else late
            rows = pl.ds(n % SLOTS * TILE, TILE)
            copies.append((source.at[rows], vertex.at[tile(head(spots, n))]))
        waited(moved(copies, sems, 2))
        waited(kept)

    @pl.when(odd == 1)
    def odd_group():
        copies = [
            (first, vertex.at[pl.ds(0, HALF)]),
            (second, vertex.at[pl.ds(HALF, HALF)]),
            (home, context),
        ]
        waited(moved(copies, sems))


def finish(*operands):
    return pl.pallas_call(
        finish_kernel,
        out_shape=[wide(2 * HALF), wide(HALF)],
        in_specs=[ANY] * 5,
        out_specs=[HBM, HBM],
        scratch_shapes=[
            pltpu.SMEM((8, 128), jnp.float32),
            pltpu.SemaphoreType.DMA((2 + VERT_TILES,)),
        ],
        compiler_params=pltpu.CompilerParams(vmem_limit_bytes=1024 * 1024),
    )(*operands)


def body(vertex, context, *lists):
    groups, members = lax.axis_size("outer"), lax.axis_size("inner")
    steps = lists[0].shape[0]

    def sent(array, odd, move):
        return lax.ppermute(array, AXES, route(groups, members, odd, move))

    low, high, o, c_state, v_state, own, names = first_step(vertex, context, lists)
    names = sent(names, 1, (0, 1 - steps))
    e = [sent(low, 0, (0, 1)), sent(high, 0, (0, 1))]
    o = sent(o, 1, (0, -1))

    def even_half(s, h, total, give=None, *after):
        x, total = even_step(s, h, e[h], c_state, total, own, give, after)
        if s + 1 < steps:
            e[h] = sent(x, 0, (0, 1))
        elif h:
            e[h] = sent(x, 0, (1, 0))
        else:
            swap = route(groups, members, 0, (1, 0)) + route(groups, members, 1, (-1, 0))
            e[h] = lax.ppermute(x, AXES, swap)
        return total

    def odd_whole(s, *after):
        x, *rest = odd_step(steps - 1 - s, o, v_state, names, after)
        return sent(x, 1, (0, -1) if s + 1 < steps else (0, steps - 1)), *rest

    beside = (2, steps - 1)
    total = even_half(1, 0, None)
    c_state = even_half(1, 1, total)
    total = even_half(2, 0, None)
    c_state = even_half(2, 1, total)
    o, v_state = odd_whole(1)
    o, v_state, early = odd_whole(2)
    early = sent(early, 1, beside)
    o, late = odd_whole(3)
    total = even_half(3, 0, None, early, late)
    late = sent(late, 1, (1, steps - 1))
    c_state = even_half(3, 1, total, None, o)
    return tuple(finish(*e, late, c_state, o))


def solution(mesh):
    return jax.shard_map(
        body,
        mesh=mesh,
        in_specs=(
            P(AXES, None),
            P(AXES, None),
            P(AXES),
            P(AXES, None),
            P(AXES, None),
            P(AXES, None, None),
            P(AXES, None, None, None),
        ),
        out_specs=(P(AXES, None), P(AXES, None)),
        check_vma=False,
    )
```

```python
import jax
import jax.numpy as jnp
from jax import lax
from jax.experimental import pallas as pl
from jax.experimental.pallas import tpu as pltpu
from jax.sharding import PartitionSpec as P

TILE = 256
WIDTH = 128
SLOTS = 8
NEG = 4
AXES = ("outer", "inner")
META = 40
SIDE = 48
LISTED = 96
VERT_TILES = 16
CTX_TILES = 8
HALF = 8 * TILE
QUARTER = 4 * TILE
FIRST_LIMIT = 60 * 1024 * 1024
STEP_LIMIT = 20 * 1024 * 1024

ANY = pl.BlockSpec(memory_space=pl.ANY)
HBM = pl.BlockSpec(memory_space=pltpu.HBM)


def route(groups, members, odd, move):
    pairs = []
    for o in range(odd, groups, 2):
        for i in range(members):
            to = ((o + move[0]) % groups) * members + (i + move[1]) % members
            pairs.append((o * members + i, to))
    return pairs


def wide(rows):
    return jax.ShapeDtypeStruct((rows, WIDTH), jnp.float32)


def vmem(rows):
    return pltpu.VMEM((rows, WIDTH), jnp.float32)


def tile(n):
    return pl.ds(pl.multiple_of(n * TILE, TILE), TILE)


def started(copies):
    for copy in copies:
        copy.start()
    return copies


def waited(copies):
    for copy in copies:
        copy.wait()


def moved(pairs, sems, first=0):
    return started(
        [
            pltpu.make_async_copy(source, to, sems.at[first + n])
            for n, (source, to) in enumerate(pairs)
        ]
    )


def halves(x):
    high = x.astype(jnp.bfloat16)
    return high, (x - high.astype(jnp.float32)).astype(jnp.bfloat16)


def dot(a, b, dims):
    return lax.dot_general(a, b, (dims, ((), ())), preferred_element_type=jnp.float32)


def slot_update(v, c, pos_row, neg_rows, live):
    v_hi, v_lo = halves(v)
    c_hi, c_lo = halves(c)
    c_both = jnp.concatenate([c_hi, c_lo], axis=1)
    v_both = jnp.concatenate([v_hi, v_lo], axis=1)
    scores = dot(
        jnp.concatenate([c_hi, c_lo, c_hi], axis=1),
        jnp.concatenate([v_hi, v_hi, v_lo], axis=1),
        ((1,), (1,)),
    )
    column = lax.broadcasted_iota(jnp.int32, (TILE, TILE), 0)
    at_pos = pos_row == column
    quarter = jnp.where(live, -0.25, 0.0)
    scale = jnp.where(at_pos, quarter, 0.0)
    for row in neg_rows:
        scale = scale + jnp.where(row == column, quarter, 0.0)
    grad = scale * jnp.tanh(0.5 * scores) + (scale + jnp.where(at_pos, -2.0 * quarter, 0.0))
    g_hi, g_lo = halves(grad)
    dc = dot(
        jnp.concatenate([g_hi, g_lo], axis=1),
        jnp.concatenate([v_both, v_both], axis=0),
        ((1,), (0,)),
    )
    dv = dot(
        jnp.concatenate([g_hi, g_lo], axis=0),
        jnp.concatenate([c_both, c_both], axis=0),
        ((0,), (0,)),
    )
    return dv[:, :WIDTH] + dv[:, WIDTH:], dc[:, :WIDTH] + dc[:, WIDTH:]


def choose(chosen, count, here):
    mine = jnp.int32(0)
    for t in range(SLOTS):
        chosen[mine] = t
        mine = mine + ((t < count) & here(t)).astype(jnp.int32)
    return mine


def run_pairs(chosen, mine, one):
    def pair(n, carry):
        results = []
        for at in (2 * n, 2 * n + 1):
            live = at < mine
            results.append(one(chosen[jnp.where(live, at, 0)], live))
        for v_to, vi, dv, c_to, ci, dc in results:
            v_to[tile(vi), :] += dv
            c_to[tile(ci), :] += dc
        return carry

    lax.fori_loop(0, (mine + 1) // 2, pair, 0)


def group_odd():
    return lax.rem(lax.axis_index("outer"), 2)


def first_kernel(steps, *refs):
    vertex, context, count_in, vert_in, ctx_in, pos_in, neg_in, *refs = refs
    low_out, high_out, moved_out, moved_high, ctx_out, vert_out, own_out, *refs = refs
    v_old, v_new, c_old, c_new, count, vert, ctx, pos, neg, own, chosen, sems = refs
    heads = moved([(count_in, count), (vert_in, vert), (ctx_in, ctx)], sems)
    lists = moved([(pos_in, pos), (neg_in, neg)], sems, 3)
    loads = moved([(context, c_old), (vertex, v_old)], sems, 5)
    waited(heads)
    mine = choose(chosen, count[0], lambda t: True)
    waited(lists)
    lane = lax.broadcasted_iota(jnp.int32, (8, 128), 1)
    for s in range(1, steps):
        base = LISTED * (s - 1)
        for side in (0, 1):
            lanes = slice(128 * side, 128 * side + 128)
            at = base + SIDE * side
            own[at : at + 8, :] = pos[s, :, lanes].astype(jnp.float32)
            for t in range(SLOTS):
                rows = slice(at + 8 + NEG * t, at + 8 + NEG * t + NEG)
                own[rows, :] = neg[s, t, :, lanes].astype(jnp.float32)
        meta = jnp.where(lane == 16, count[s], 0)
        for t in range(SLOTS):
            meta = jnp.where(lane == t, vert[s, t], meta)
            meta = jnp.where(lane == 8 + t, ctx[s, t], meta)
        meta = meta.astype(jnp.float32)
        own[base + META : base + SIDE, :] = meta
        own[base + SIDE + META : base + LISTED, :] = meta
    waited(loads)

    def fill(n, carry):
        c_new[tile(n), :] = c_old[tile(n), :]
        v_new[tile(2 * n), :] = v_old[tile(2 * n), :]
        v_new[tile(2 * n + 1), :] = v_old[tile(2 * n + 1), :]
        return carry

    lax.fori_loop(0, CTX_TILES, fill, 0)

    def one(t, live):
        vi, ci = vert[0, t], ctx[0, t]
        rows = [neg[0, t, pl.ds(k, 1), :] for k in range(NEG)]
        pos_row = pos[0, pl.ds(t, 1), :]
        dv, dc = slot_update(v_old[tile(vi), :], c_old[tile(ci), :], pos_row, rows, live)
        return v_new, vi, dv, c_new, ci, dc

    run_pairs(chosen, mine, one)
    odd = group_odd()

    @pl.when(odd == 0)
    def even_group():
        stores = [
            (v_new.at[pl.ds(0, HALF)], low_out),
            (v_new.at[pl.ds(HALF, HALF)], high_out),
            (c_new, ctx_out),
            (own, own_out),
        ]
        waited(moved(stores, sems))

    @pl.when(odd == 1)
    def odd_group():
        stores = [
            (c_new.at[pl.ds(0, QUARTER)], moved_out.at[pl.ds(0, QUARTER)]),
            (own, moved_out.at[pl.ds(QUARTER, LISTED * (steps - 1))]),
            (c_new.at[pl.ds(QUARTER, QUARTER)], moved_high),
            (v_new, vert_out),
        ]
        waited(moved(stores, sems))


def first_step(vertex, context, lists):
    steps = lists[0].shape[0]
    listed = LISTED * (steps - 1)

    def kernel(*refs):
        first_kernel(steps, *refs)

    return pl.pallas_call(
        kernel,
        out_shape=[
            wide(HALF),
            wide(HALF),
            wide(QUARTER + listed),
            wide(QUARTER),
            wide(HALF),
            wide(2 * HALF),
            wide(listed),
        ],
        in_specs=[ANY] * 7,
        out_specs=[ANY] * 7,
        scratch_shapes=[
            vmem(2 * HALF),
            vmem(2 * HALF),
            vmem(HALF),
            vmem(HALF),
            pltpu.SMEM((steps,), jnp.int32),
            pltpu.SMEM((steps, SLOTS), jnp.int32),
            pltpu.SMEM((steps, SLOTS), jnp.int32),
            pltpu.VMEM((steps, SLOTS, TILE), jnp.int32),
            pltpu.VMEM((steps, SLOTS, NEG, TILE), jnp.int32),
            vmem(listed),
            pltpu.SMEM((SLOTS + 1,), jnp.int32),
            pltpu.SemaphoreType.DMA((7,)),
        ],
        compiler_params=pltpu.CompilerParams(vmem_limit_bytes=FIRST_LIMIT),
        cost_estimate=pl.CostEstimate(flops=1000, bytes_accessed=1000, transcendentals=0),
    )(vertex, context, *lists)


def head(meta, lane):
    return meta[0, lane].astype(jnp.int32)


def listed_rows(listed, t):
    def row(r):
        both = [listed[pl.ds(r, 1), :], listed[pl.ds(SIDE + r, 1), :]]
        return jnp.concatenate(both, axis=1).astype(jnp.int32)

    return row(t), [row(8 + NEG * t + k) for k in range(NEG)]


def even_kernel(s, half, joined, swaps, n_after, *refs):
    move_in, stay_in, *refs = refs
    total_in = stay_in
    if joined:
        total_in, *refs = refs
    own, *refs = refs
    if swaps:
        give, *refs = refs
    move_out, stay_out, *refs = refs[n_after:]
    m_old, m_new, s_old, s_new, listed, meta, chosen, sems = refs
    if swaps:

        @pl.when(group_odd() == 1)
        def hand_on():
            waited(moved([(give, move_out)], sems))

    @pl.when(group_odd() == 0)
    def work():
        list_in = own.at[pl.ds(LISTED * (s - 1), LISTED)]
        heads = moved([(list_in.at[pl.ds(META, 8)], meta)], sems)
        loads = [
            (list_in, listed),
            (move_in, m_old),
            (stay_in, s_old),
            (move_in, m_new),
            (total_in, s_new),
        ]
        loads = moved(loads, sems, 1)
        waited(heads)
        mine = choose(chosen, head(meta, 16), lambda t: head(meta, t) // 8 == half)
        waited(loads)

        def one(t, live):
            vi, ci = lax.rem(head(meta, t), 8), head(meta, 8 + t)
            rows = listed_rows(listed, t)
            dv, dc = slot_update(m_old[tile(vi), :], s_old[tile(ci), :], *rows, live)
            return m_new, vi, dv, s_new, ci, dc

        run_pairs(chosen, mine, one)
        stores = [(m_new, move_out.at[pl.ds(0, HALF)]), (s_new, stay_out)]
        waited(moved(stores, sems))


def even_step(s, half, moving, staying, total, own, give, after):
    swaps = give is not None
    operands = [moving, staying] + ([] if total is None else [total]) + [own]
    operands += ([give] if swaps else []) + [*after]
    size = give.shape[0] if swaps else HALF

    def kernel(*refs):
        even_kernel(s, half, total is not None, swaps, len(after), *refs)

    return pl.pallas_call(
        kernel,
        out_shape=[wide(size), wide(HALF)],
        in_specs=[ANY] * len(operands),
        out_specs=[ANY, ANY],
        scratch_shapes=[
            vmem(HALF),
            vmem(HALF),
            vmem(HALF),
            vmem(HALF),
            vmem(LISTED),
            pltpu.SMEM((8, 128), jnp.float32),
            pltpu.SMEM((SLOTS + 1,), jnp.int32),
            pltpu.SemaphoreType.DMA((6,)),
        ],
        compiler_params=pltpu.CompilerParams(vmem_limit_bytes=STEP_LIMIT),
        cost_estimate=pl.CostEstimate(flops=1000, bytes_accessed=1000, transcendentals=0),
    )(*operands)


def part_tiles(meta, used, order):
    for n in range(VERT_TILES):
        used[n] = 0
    for t in range(SLOTS):
        at = head(meta, t)
        used[at] = jnp.where(t < head(meta, 16), 1, used[at])
    early, late = jnp.int32(0), jnp.int32(SLOTS)
    for n in range(VERT_TILES):
        soon = (used[n] == 0) & (early < SLOTS)
        order[jnp.where(soon, early, late)] = n
        early = early + soon.astype(jnp.int32)
        late = late + 1 - soon.astype(jnp.int32)


def odd_kernel(left, half, n_after, *refs):
    move_in, stay_in, *refs = refs
    list_in, total_in = move_in.at[pl.ds(QUARTER, LISTED)] if not half else None, stay_in
    parts = left == 0
    if half:
        carrier, total_in, *refs = refs
        list_in = carrier.at[pl.ds(QUARTER, LISTED)]
    refs = refs[n_after:]
    move_out, *refs = refs
    if left or not half:
        stay_out, *refs = refs
    if parts:
        part_out, *refs = refs
    m_old, m_new, s_old, s_new, listed, meta, chosen, used, order, places, sems = refs

    @pl.when(group_odd() == 1)
    def work():
        heads = moved([(list_in.at[pl.ds(META, 8)], meta)], sems)
        loads = [
            (list_in, listed),
            (move_in.at[pl.ds(0, QUARTER)], m_old),
            (stay_in, s_old),
            (move_in.at[pl.ds(0, QUARTER)], m_new),
            (total_in, s_new),
        ]
        if left and not half:
            rest = pl.ds(QUARTER, LISTED * left)
            loads.append((move_in.at[pl.ds(QUARTER + LISTED, LISTED * left)], move_out.at[rest]))
        loads = moved(loads, sems, 2)
        waited(heads)
        mine = choose(chosen, head(meta, 16), lambda t: head(meta, 8 + t) // 4 == half)
        if parts:
            part_tiles(meta, used, order)
        waited(loads)

        def one(t, live):
            vi, ci = head(meta, t), lax.rem(head(meta, 8 + t), 4)
            rows = listed_rows(listed, t)
            dv, dc = slot_update(s_old[tile(vi), :], m_old[tile(ci), :], *rows, live)
            return s_new, vi, dv, m_new, ci, dc

        run_pairs(chosen, mine, one)
        stores = [(m_new, move_out.at[pl.ds(0, QUARTER)])]
        if left or not half:
            stores.append((s_new, stay_out))
        if parts:
            first = SLOTS if half else 0
            stores += [
                (s_new.at[tile(order[first + n])], part_out.at[pl.ds(n * TILE, TILE)])
                for n in range(SLOTS)
            ]
        if parts and half:
            lane = lax.broadcasted_iota(jnp.int32, (8, 128), 1)
            spot = jnp.zeros((8, 128), jnp.int32)
            for n in range(VERT_TILES):
                spot = jnp.where(lane == n, order[n], spot)
            places[...] = spot.astype(jnp.float32)
            stores.append((places, part_out.at[pl.ds(HALF, 8)]))
        waited(moved(stores, sems))


def odd_step(left, half, moving, staying, carrier, total, after):
    operands = [moving, staying]
    out_shape = [wide(QUARTER + (0 if half else LISTED * left))]
    if left or not half:
        out_shape.append(wide(2 * HALF))
    if half:
        operands += [carrier, total]
    if left == 0:
        out_shape.append(wide(HALF + 8 if half else HALF))

    def kernel(*refs):
        odd_kernel(left, half, len(after), *refs)

    return pl.pallas_call(
        kernel,
        out_shape=out_shape,
        in_specs=[ANY] * (len(operands) + len(after)),
        out_specs=[ANY] * len(out_shape),
        scratch_shapes=[
            vmem(QUARTER),
            vmem(QUARTER),
            vmem(2 * HALF),
            vmem(2 * HALF),
            vmem(LISTED),
            pltpu.SMEM((8, 128), jnp.float32),
            pltpu.SMEM((SLOTS + 1,), jnp.int32),
            pltpu.SMEM((VERT_TILES,), jnp.int32),
            pltpu.SMEM((VERT_TILES,), jnp.int32),
            vmem(8),
            pltpu.SemaphoreType.DMA((12,)),
        ],
        compiler_params=pltpu.CompilerParams(vmem_limit_bytes=STEP_LIMIT),
        cost_estimate=pl.CostEstimate(flops=4000000000, bytes_accessed=1000, transcendentals=0),
    )(*operands, *after)


def finish_kernel(first, second, late, stayed, home, home_high, vertex, context, spots, sems):
    odd = group_odd()

    @pl.when(odd == 0)
    def even_group():
        heads = moved([(late.at[pl.ds(HALF, 8)], spots)], sems)
        kept = moved([(stayed, context)], sems, 1)
        waited(heads)
        copies = []
        for n in range(VERT_TILES):
            source = first if n < SLOTS else late
            rows = pl.ds(n % SLOTS * TILE, TILE)
            copies.append((source.at[rows], vertex.at[tile(head(spots, n))]))
        waited(moved(copies, sems, 2))
        waited(kept)

    @pl.when(odd == 1)
    def odd_group():
        copies = [
            (first, vertex.at[pl.ds(0, HALF)]),
            (second, vertex.at[pl.ds(HALF, HALF)]),
            (home, context.at[pl.ds(0, QUARTER)]),
            (home_high, context.at[pl.ds(QUARTER, QUARTER)]),
        ]
        waited(moved(copies, sems))


def finish(*operands):
    return pl.pallas_call(
        finish_kernel,
        out_shape=[wide(2 * HALF), wide(HALF)],
        in_specs=[ANY] * 6,
        out_specs=[HBM, HBM],
        scratch_shapes=[
            pltpu.SMEM((8, 128), jnp.float32),
            pltpu.SemaphoreType.DMA((2 + VERT_TILES,)),
        ],
        compiler_params=pltpu.CompilerParams(vmem_limit_bytes=1024 * 1024),
    )(*operands)


def body(vertex, context, *lists):
    groups, members = lax.axis_size("outer"), lax.axis_size("inner")
    steps = lists[0].shape[0]

    def sent(array, odd, move):
        return lax.ppermute(array, AXES, route(groups, members, odd, move))

    low, high, *o, c_state, v_state, own = first_step(vertex, context, lists)
    e = [sent(low, 0, (0, 1)), sent(high, 0, (0, 1))]
    o = [sent(x, 1, (0, -1)) for x in o]

    def even_half(s, h, total, give=None, *after):
        x, total = even_step(s, h, e[h], c_state, total, own, give, after)
        if s + 1 < steps:
            e[h] = sent(x, 0, (0, 1))
        elif h:
            e[h] = sent(x, 0, (1, 0))
        else:
            swap = route(groups, members, 0, (1, 0)) + route(groups, members, 1, (-1, 0))
            e[h] = lax.ppermute(x, AXES, swap)
        return total

    def odd_half(s, h, total, *after):
        carrier = None if h == 0 else carriers[s]
        carriers[s] = o[h] if h == 0 else carrier
        x, *rest = odd_step(steps - 1 - s, h, o[h], v_state, carrier, total, after)
        o[h] = sent(x, 1, (0, -1) if s + 1 < steps else (0, steps - 1))
        return rest

    carriers = {}
    beside = (2, steps - 1)
    total = even_half(1, 0, None)
    c_state = even_half(1, 1, total)
    total = even_half(2, 0, None)
    c_state = even_half(2, 1, total)
    (v_state,) = odd_half(1, 1, *odd_half(1, 0, None))
    (v_state,) = odd_half(2, 1, *odd_half(2, 0, None))
    total, early = odd_half(3, 0, None)
    early = sent(early, 1, beside)
    (late,) = odd_half(3, 1, total)
    total = even_half(3, 0, None, early, late)
    late = sent(late, 1, (1, steps - 1))
    c_state = even_half(3, 1, total, None, *o)
    return tuple(finish(*e, late, c_state, *o))


def solution(mesh):
    return jax.shard_map(
        body,
        mesh=mesh,
        in_specs=(
            P(AXES, None),
            P(AXES, None),
            P(AXES),
            P(AXES, None),
            P(AXES, None),
            P(AXES, None, None),
            P(AXES, None, None, None),
        ),
        out_specs=(P(AXES, None), P(AXES, None)),
        check_vma=False,
    )
```

```python
import jax
import jax.numpy as jnp
from jax import lax
from jax.experimental import pallas as pl
from jax.experimental.pallas import tpu as pltpu
from jax.sharding import PartitionSpec as P

TILE = 256
WIDTH = 128
SLOTS = 8
NEG = 4
AXES = ("outer", "inner")
META = 40
SIDE = 48
LISTED = 96
VERT_TILES = 16
CTX_TILES = 8
HALF = 8 * TILE
QUARTER = 4 * TILE
FIRST_LIMIT = 60 * 1024 * 1024
STEP_LIMIT = 20 * 1024 * 1024

ANY = pl.BlockSpec(memory_space=pl.ANY)
HBM = pl.BlockSpec(memory_space=pltpu.HBM)


def route(groups, members, odd, move):
    pairs = []
    for o in range(odd, groups, 2):
        for i in range(members):
            to = ((o + move[0]) % groups) * members + (i + move[1]) % members
            pairs.append((o * members + i, to))
    return pairs


def wide(rows):
    return jax.ShapeDtypeStruct((rows, WIDTH), jnp.float32)


def vmem(rows):
    return pltpu.VMEM((rows, WIDTH), jnp.float32)


def tile(n):
    return pl.ds(pl.multiple_of(n * TILE, TILE), TILE)


def started(copies):
    for copy in copies:
        copy.start()
    return copies


def waited(copies):
    for copy in copies:
        copy.wait()


def moved(pairs, sems, first=0):
    return started(
        [
            pltpu.make_async_copy(source, to, sems.at[first + n])
            for n, (source, to) in enumerate(pairs)
        ]
    )


def halves(x):
    high = x.astype(jnp.bfloat16)
    return high, (x - high.astype(jnp.float32)).astype(jnp.bfloat16)


def dot(a, b, dims):
    return lax.dot_general(a, b, (dims, ((), ())), preferred_element_type=jnp.float32)


def slot_update(v, c, pos_row, neg_rows, live):
    v_hi, v_lo = halves(v)
    c_hi, c_lo = halves(c)
    c_both = jnp.concatenate([c_hi, c_lo], axis=1)
    v_both = jnp.concatenate([v_hi, v_lo], axis=1)
    scores = dot(
        jnp.concatenate([c_hi, c_lo, c_hi], axis=1),
        jnp.concatenate([v_hi, v_hi, v_lo], axis=1),
        ((1,), (1,)),
    )
    column = lax.broadcasted_iota(jnp.int32, (TILE, TILE), 0)
    at_pos = pos_row == column
    quarter = jnp.where(live, -0.25, 0.0)
    scale = jnp.where(at_pos, quarter, 0.0)
    for row in neg_rows:
        scale = scale + jnp.where(row == column, quarter, 0.0)
    grad = scale * jnp.tanh(0.5 * scores) + (scale + jnp.where(at_pos, -2.0 * quarter, 0.0))
    g_hi, g_lo = halves(grad)
    dc = dot(
        jnp.concatenate([g_hi, g_lo], axis=1),
        jnp.concatenate([v_both, v_both], axis=0),
        ((1,), (0,)),
    )
    dv = dot(
        jnp.concatenate([g_hi, g_lo], axis=0),
        jnp.concatenate([c_both, c_both], axis=0),
        ((0,), (0,)),
    )
    return dv[:, :WIDTH] + dv[:, WIDTH:], dc[:, :WIDTH] + dc[:, WIDTH:]


def choose(chosen, count, here):
    mine = jnp.int32(0)
    for t in range(SLOTS):
        chosen[mine] = t
        mine = mine + ((t < count) & here(t)).astype(jnp.int32)
    return mine


def run_pairs(chosen, mine, one):
    def pair(n, carry):
        results = []
        for at in (2 * n, 2 * n + 1):
            live = at < mine
            results.append(one(chosen[jnp.where(live, at, 0)], live))
        for v_to, vi, dv, c_to, ci, dc in results:
            v_to[tile(vi), :] += dv
            c_to[tile(ci), :] += dc
        return carry

    lax.fori_loop(0, (mine + 1) // 2, pair, 0)


def group_odd():
    return lax.rem(lax.axis_index("outer"), 2)


def first_kernel(steps, *refs):
    vertex, context, count_in, vert_in, ctx_in, pos_in, neg_in, *refs = refs
    low_out, high_out, moved_out, moved_high, ctx_out, vert_out, own_out, *refs = refs
    v_old, v_new, c_old, c_new, count, vert, ctx, pos, neg, own, chosen, sems = refs
    heads = moved([(count_in, count), (vert_in, vert), (ctx_in, ctx)], sems)
    lists = moved([(pos_in, pos), (neg_in, neg)], sems, 3)
    loads = moved([(context, c_old), (vertex, v_old)], sems, 5)
    waited(heads)
    mine = choose(chosen, count[0], lambda t: True)
    waited(lists)
    lane = lax.broadcasted_iota(jnp.int32, (8, 128), 1)
    for s in range(1, steps):
        base = LISTED * (s - 1)
        for side in (0, 1):
            lanes = slice(128 * side, 128 * side + 128)
            at = base + SIDE * side
            own[at : at + 8, :] = pos[s, :, lanes].astype(jnp.float32)
            for t in range(SLOTS):
                rows = slice(at + 8 + NEG * t, at + 8 + NEG * t + NEG)
                own[rows, :] = neg[s, t, :, lanes].astype(jnp.float32)
        meta = jnp.where(lane == 16, count[s], 0)
        for t in range(SLOTS):
            meta = jnp.where(lane == t, vert[s, t], meta)
            meta = jnp.where(lane == 8 + t, ctx[s, t], meta)
        meta = meta.astype(jnp.float32)
        own[base + META : base + SIDE, :] = meta
        own[base + SIDE + META : base + LISTED, :] = meta
    waited(loads)

    def fill(n, carry):
        c_new[tile(n), :] = c_old[tile(n), :]
        v_new[tile(2 * n), :] = v_old[tile(2 * n), :]
        v_new[tile(2 * n + 1), :] = v_old[tile(2 * n + 1), :]
        return carry

    lax.fori_loop(0, CTX_TILES, fill, 0)

    def one(t, live):
        vi, ci = vert[0, t], ctx[0, t]
        rows = [neg[0, t, pl.ds(k, 1), :] for k in range(NEG)]
        pos_row = pos[0, pl.ds(t, 1), :]
        dv, dc = slot_update(v_old[tile(vi), :], c_old[tile(ci), :], pos_row, rows, live)
        return v_new, vi, dv, c_new, ci, dc

    run_pairs(chosen, mine, one)
    odd = group_odd()

    @pl.when(odd == 0)
    def even_group():
        stores = [
            (v_new.at[pl.ds(0, HALF)], low_out),
            (v_new.at[pl.ds(HALF, HALF)], high_out),
            (c_new, ctx_out),
            (own, own_out),
        ]
        waited(moved(stores, sems))

    @pl.when(odd == 1)
    def odd_group():
        stores = [
            (c_new.at[pl.ds(0, QUARTER)], moved_out.at[pl.ds(0, QUARTER)]),
            (own, moved_out.at[pl.ds(QUARTER, LISTED * (steps - 1))]),
            (c_new.at[pl.ds(QUARTER, QUARTER)], moved_high),
            (v_new, vert_out),
        ]
        waited(moved(stores, sems))


def first_step(vertex, context, lists):
    steps = lists[0].shape[0]
    listed = LISTED * (steps - 1)

    def kernel(*refs):
        first_kernel(steps, *refs)

    return pl.pallas_call(
        kernel,
        out_shape=[
            wide(HALF),
            wide(HALF),
            wide(QUARTER + listed),
            wide(QUARTER),
            wide(HALF),
            wide(2 * HALF),
            wide(listed),
        ],
        in_specs=[ANY] * 7,
        out_specs=[ANY] * 7,
        scratch_shapes=[
            vmem(2 * HALF),
            vmem(2 * HALF),
            vmem(HALF),
            vmem(HALF),
            pltpu.SMEM((steps,), jnp.int32),
            pltpu.SMEM((steps, SLOTS), jnp.int32),
            pltpu.SMEM((steps, SLOTS), jnp.int32),
            pltpu.VMEM((steps, SLOTS, TILE), jnp.int32),
            pltpu.VMEM((steps, SLOTS, NEG, TILE), jnp.int32),
            vmem(listed),
            pltpu.SMEM((SLOTS + 1,), jnp.int32),
            pltpu.SemaphoreType.DMA((7,)),
        ],
        compiler_params=pltpu.CompilerParams(vmem_limit_bytes=FIRST_LIMIT),
        cost_estimate=pl.CostEstimate(flops=1000, bytes_accessed=1000, transcendentals=0),
    )(vertex, context, *lists)


def head(meta, lane):
    return meta[0, lane].astype(jnp.int32)


def listed_rows(listed, t):
    def row(r):
        both = [listed[pl.ds(r, 1), :], listed[pl.ds(SIDE + r, 1), :]]
        return jnp.concatenate(both, axis=1).astype(jnp.int32)

    return row(t), [row(8 + NEG * t + k) for k in range(NEG)]


def even_kernel(s, half, joined, swaps, n_after, *refs):
    move_in, stay_in, *refs = refs
    total_in = stay_in
    if joined:
        total_in, *refs = refs
    own, *refs = refs
    if swaps:
        give, *refs = refs
    move_out, stay_out, *refs = refs[n_after:]
    m_old, m_new, s_old, s_new, listed, meta, chosen, sems = refs
    if swaps:

        @pl.when(group_odd() == 1)
        def hand_on():
            waited(moved([(give, move_out)], sems))

    @pl.when(group_odd() == 0)
    def work():
        list_in = own.at[pl.ds(LISTED * (s - 1), LISTED)]
        heads = moved([(list_in.at[pl.ds(META, 8)], meta)], sems)
        loads = [
            (list_in, listed),
            (move_in, m_old),
            (stay_in, s_old),
            (move_in, m_new),
            (total_in, s_new),
        ]
        loads = moved(loads, sems, 1)
        waited(heads)
        mine = choose(chosen, head(meta, 16), lambda t: head(meta, t) // 8 == half)
        waited(loads)

        def one(t, live):
            vi, ci = lax.rem(head(meta, t), 8), head(meta, 8 + t)
            rows = listed_rows(listed, t)
            dv, dc = slot_update(m_old[tile(vi), :], s_old[tile(ci), :], *rows, live)
            return m_new, vi, dv, s_new, ci, dc

        run_pairs(chosen, mine, one)
        stores = [(m_new, move_out.at[pl.ds(0, HALF)]), (s_new, stay_out)]
        waited(moved(stores, sems))


def even_step(s, half, moving, staying, total, own, give, after):
    swaps = give is not None
    operands = [moving, staying] + ([] if total is None else [total]) + [own]
    operands += ([give] if swaps else []) + [*after]
    size = give.shape[0] if swaps else HALF

    def kernel(*refs):
        even_kernel(s, half, total is not None, swaps, len(after), *refs)

    return pl.pallas_call(
        kernel,
        out_shape=[wide(size), wide(HALF)],
        in_specs=[ANY] * len(operands),
        out_specs=[ANY, ANY],
        scratch_shapes=[
            vmem(HALF),
            vmem(HALF),
            vmem(HALF),
            vmem(HALF),
            vmem(LISTED),
            pltpu.SMEM((8, 128), jnp.float32),
            pltpu.SMEM((SLOTS + 1,), jnp.int32),
            pltpu.SemaphoreType.DMA((6,)),
        ],
        compiler_params=pltpu.CompilerParams(vmem_limit_bytes=STEP_LIMIT),
        cost_estimate=pl.CostEstimate(flops=1000, bytes_accessed=1000, transcendentals=0),
    )(*operands)


def part_tiles(meta, used, order):
    for n in range(VERT_TILES):
        used[n] = 0
    for t in range(SLOTS):
        at = head(meta, t)
        used[at] = jnp.where(t < head(meta, 16), 1, used[at])
    early, late = jnp.int32(0), jnp.int32(SLOTS)
    for n in range(VERT_TILES):
        soon = (used[n] == 0) & (early < SLOTS)
        order[jnp.where(soon, early, late)] = n
        early = early + soon.astype(jnp.int32)
        late = late + 1 - soon.astype(jnp.int32)


def odd_kernel(left, half, n_after, *refs):
    move_in, stay_in, *refs = refs
    list_in, total_in = move_in.at[pl.ds(QUARTER, LISTED)] if not half else None, stay_in
    parts = left == 0
    if half:
        carrier, total_in, *refs = refs
        list_in = carrier.at[pl.ds(QUARTER, LISTED)]
    refs = refs[n_after:]
    move_out, *refs = refs
    if left or not half:
        stay_out, *refs = refs
    if parts:
        part_out, *refs = refs
    m_old, m_new, s_old, s_new, listed, meta, chosen, used, order, places, sems = refs

    @pl.when(group_odd() == 1)
    def work():
        heads = moved([(list_in.at[pl.ds(META, 8)], meta)], sems)
        loads = [
            (list_in, listed),
            (move_in.at[pl.ds(0, QUARTER)], m_old),
            (stay_in, s_old),
            (move_in.at[pl.ds(0, QUARTER)], m_new),
            (total_in, s_new),
        ]
        if left and not half:
            rest = pl.ds(QUARTER, LISTED * left)
            loads.append((move_in.at[pl.ds(QUARTER + LISTED, LISTED * left)], move_out.at[rest]))
        loads = moved(loads, sems, 2)
        waited(heads)
        mine = choose(chosen, head(meta, 16), lambda t: head(meta, 8 + t) // 4 == half)
        if parts:
            part_tiles(meta, used, order)
        waited(loads)

        def one(t, live):
            vi, ci = head(meta, t), lax.rem(head(meta, 8 + t), 4)
            rows = listed_rows(listed, t)
            dv, dc = slot_update(s_old[tile(vi), :], m_old[tile(ci), :], *rows, live)
            return s_new, vi, dv, m_new, ci, dc

        run_pairs(chosen, mine, one)
        stores = [(m_new, move_out.at[pl.ds(0, QUARTER)])]
        if left or not half:
            stores.append((s_new, stay_out))
        if parts:
            first = SLOTS if half else 0
            stores += [
                (s_new.at[tile(order[first + n])], part_out.at[pl.ds(n * TILE, TILE)])
                for n in range(SLOTS)
            ]
        if parts and half:
            lane = lax.broadcasted_iota(jnp.int32, (8, 128), 1)
            spot = jnp.zeros((8, 128), jnp.int32)
            for n in range(VERT_TILES):
                spot = jnp.where(lane == n, order[n], spot)
            places[...] = spot.astype(jnp.float32)
            stores.append((places, part_out.at[pl.ds(HALF, 8)]))
        waited(moved(stores, sems))


def odd_step(left, half, moving, staying, carrier, total, after):
    operands = [moving, staying]
    out_shape = [wide(QUARTER + (0 if half else LISTED * left))]
    if left or not half:
        out_shape.append(wide(2 * HALF))
    if half:
        operands += [carrier, total]
    if left == 0:
        out_shape.append(wide(HALF + 8 if half else HALF))

    def kernel(*refs):
        odd_kernel(left, half, len(after), *refs)

    return pl.pallas_call(
        kernel,
        out_shape=out_shape,
        in_specs=[ANY] * (len(operands) + len(after)),
        out_specs=[ANY] * len(out_shape),
        scratch_shapes=[
            vmem(QUARTER),
            vmem(QUARTER),
            vmem(2 * HALF),
            vmem(2 * HALF),
            vmem(LISTED),
            pltpu.SMEM((8, 128), jnp.float32),
            pltpu.SMEM((SLOTS + 1,), jnp.int32),
            pltpu.SMEM((VERT_TILES,), jnp.int32),
            pltpu.SMEM((VERT_TILES,), jnp.int32),
            vmem(8),
            pltpu.SemaphoreType.DMA((12,)),
        ],
        compiler_params=pltpu.CompilerParams(vmem_limit_bytes=STEP_LIMIT),
        cost_estimate=pl.CostEstimate(flops=4000000000, bytes_accessed=1000, transcendentals=0),
    )(*operands, *after)


def finish_kernel(first, second, late, stayed, home, home_high, vertex, context, spots, sems):
    odd = group_odd()

    @pl.when(odd == 0)
    def even_group():
        heads = moved([(late.at[pl.ds(HALF, 8)], spots)], sems)
        kept = moved([(stayed, context)], sems, 1)
        waited(heads)
        copies = []
        for n in range(VERT_TILES):
            source = second if n < SLOTS else late
            rows = pl.ds(n % SLOTS * TILE, TILE)
            copies.append((source.at[rows], vertex.at[tile(head(spots, n))]))
        waited(moved(copies, sems, 2))
        waited(kept)

    @pl.when(odd == 1)
    def odd_group():
        copies = [
            (first, vertex.at[pl.ds(0, HALF)]),
            (second, vertex.at[pl.ds(HALF, HALF)]),
            (home, context.at[pl.ds(0, QUARTER)]),
            (home_high, context.at[pl.ds(QUARTER, QUARTER)]),
        ]
        waited(moved(copies, sems))


def finish(*operands):
    return pl.pallas_call(
        finish_kernel,
        out_shape=[wide(2 * HALF), wide(HALF)],
        in_specs=[ANY] * 6,
        out_specs=[HBM, HBM],
        scratch_shapes=[
            pltpu.SMEM((8, 128), jnp.float32),
            pltpu.SemaphoreType.DMA((2 + VERT_TILES,)),
        ],
        compiler_params=pltpu.CompilerParams(vmem_limit_bytes=1024 * 1024),
    )(*operands)


def body(vertex, context, *lists):
    groups, members = lax.axis_size("outer"), lax.axis_size("inner")
    steps = lists[0].shape[0]

    def sent(array, odd, move):
        return lax.ppermute(array, AXES, route(groups, members, odd, move))

    low, high, *o, c_state, v_state, own = first_step(vertex, context, lists)
    e = [sent(low, 0, (0, 1)), sent(high, 0, (0, 1))]
    o = [sent(x, 1, (0, -1)) for x in o]

    def even_half(s, h, total, give=None, *after):
        x, total = even_step(s, h, e[h], c_state, total, own, give, after)
        if s + 1 < steps:
            e[h] = sent(x, 0, (0, 1))
        elif give is None:
            e[h] = sent(x, 0, (1, 0))
        else:
            swap = route(groups, members, 0, (1, 0)) + route(groups, members, 1, (-1, 0))
            e[h] = lax.ppermute(x, AXES, swap)
        return total

    def odd_half(s, h, total, *after):
        carrier = None if h == 0 else carriers[s]
        carriers[s] = o[h] if h == 0 else carrier
        x, *rest = odd_step(steps - 1 - s, h, o[h], v_state, carrier, total, after)
        o[h] = sent(x, 1, (0, -1) if s + 1 < steps else (0, steps - 1))
        return rest

    carriers = {}
    beside = (2, steps - 1)
    total = even_half(1, 0, None)
    c_state = even_half(1, 1, total)
    total = even_half(2, 0, None)
    c_state = even_half(2, 1, total)
    (v_state,) = odd_half(1, 1, *odd_half(1, 0, None))
    (v_state,) = odd_half(2, 1, *odd_half(2, 0, None))
    total, early = odd_half(3, 0, None)
    early = sent(early, 1, beside)
    (late,) = odd_half(3, 1, total)
    total = even_half(3, 0, None, None, late)
    late = sent(late, 1, (1, steps - 1))
    c_state = even_half(3, 1, total, early, *o)
    return tuple(finish(*e, late, c_state, *o))


def solution(mesh):
    return jax.shard_map(
        body,
        mesh=mesh,
        in_specs=(
            P(AXES, None),
            P(AXES, None),
            P(AXES),
            P(AXES, None),
            P(AXES, None),
            P(AXES, None, None),
            P(AXES, None, None, None),
        ),
        out_specs=(P(AXES, None), P(AXES, None)),
        check_vma=False,
    )
```

```python
import jax
import jax.numpy as jnp
from jax import lax
from jax.experimental import pallas as pl
from jax.experimental.pallas import tpu as pltpu
from jax.sharding import PartitionSpec as P

TILE = 256
WIDTH = 128
SLOTS = 8
NEG = 4
AXES = ("outer", "inner")
META = 40
SIDE = 48
LISTED = 96
VERT_TILES = 16
CTX_TILES = 8
HALF = 8 * TILE
QUARTER = 4 * TILE
FIRST_LIMIT = 60 * 1024 * 1024
STEP_LIMIT = 20 * 1024 * 1024

ANY = pl.BlockSpec(memory_space=pl.ANY)
HBM = pl.BlockSpec(memory_space=pltpu.HBM)


def route(groups, members, odd, move):
    pairs = []
    for o in range(odd, groups, 2):
        for i in range(members):
            to = ((o + move[0]) % groups) * members + (i + move[1]) % members
            pairs.append((o * members + i, to))
    return pairs


def wide(rows):
    return jax.ShapeDtypeStruct((rows, WIDTH), jnp.float32)


def vmem(rows):
    return pltpu.VMEM((rows, WIDTH), jnp.float32)


def tile(n):
    return pl.ds(pl.multiple_of(n * TILE, TILE), TILE)


def started(copies):
    for copy in copies:
        copy.start()
    return copies


def waited(copies):
    for copy in copies:
        copy.wait()


def moved(pairs, sems, first=0):
    return started(
        [
            pltpu.make_async_copy(source, to, sems.at[first + n])
            for n, (source, to) in enumerate(pairs)
        ]
    )


def halves(x):
    high = x.astype(jnp.bfloat16)
    return high, (x - high.astype(jnp.float32)).astype(jnp.bfloat16)


def dot(a, b, dims):
    return lax.dot_general(a, b, (dims, ((), ())), preferred_element_type=jnp.float32)


def slot_update(v, c, pos_row, neg_rows, live):
    v_hi, v_lo = halves(v)
    c_hi, c_lo = halves(c)
    c_both = jnp.concatenate([c_hi, c_lo], axis=1)
    v_both = jnp.concatenate([v_hi, v_lo], axis=1)
    scores = dot(
        jnp.concatenate([c_hi, c_lo, c_hi], axis=1),
        jnp.concatenate([v_hi, v_hi, v_lo], axis=1),
        ((1,), (1,)),
    )
    column = lax.broadcasted_iota(jnp.int32, (TILE, TILE), 0)
    at_pos = pos_row == column
    quarter = jnp.where(live, -0.25, 0.0)
    scale = jnp.where(at_pos, quarter, 0.0)
    for row in neg_rows:
        scale = scale + jnp.where(row == column, quarter, 0.0)
    grad = scale * jnp.tanh(0.5 * scores) + (scale + jnp.where(at_pos, -2.0 * quarter, 0.0))
    g_hi, g_lo = halves(grad)
    dc = dot(
        jnp.concatenate([g_hi, g_lo], axis=1),
        jnp.concatenate([v_both, v_both], axis=0),
        ((1,), (0,)),
    )
    dv = dot(
        jnp.concatenate([g_hi, g_lo], axis=0),
        jnp.concatenate([c_both, c_both], axis=0),
        ((0,), (0,)),
    )
    return dv[:, :WIDTH] + dv[:, WIDTH:], dc[:, :WIDTH] + dc[:, WIDTH:]


def choose(chosen, count, here):
    mine = jnp.int32(0)
    for t in range(SLOTS):
        chosen[mine] = t
        mine = mine + ((t < count) & here(t)).astype(jnp.int32)
    return mine


def run_pairs(chosen, mine, one):
    def pair(n, carry):
        results = []
        for at in (2 * n, 2 * n + 1):
            live = at < mine
            results.append(one(chosen[jnp.where(live, at, 0)], live))
        for v_to, vi, dv, c_to, ci, dc in results:
            v_to[tile(vi), :] += dv
            c_to[tile(ci), :] += dc
        return carry

    lax.fori_loop(0, (mine + 1) // 2, pair, 0)


def group_odd():
    return lax.rem(lax.axis_index("outer"), 2)


def first_kernel(steps, *refs):
    vertex, context, count_in, vert_in, ctx_in, pos_in, neg_in, *refs = refs
    low_out, high_out, moved_out, moved_high, ctx_out, vert_out, own_out, *refs = refs
    v_old, v_new, c_old, c_new, count, vert, ctx, pos, neg, own, chosen, sems = refs
    heads = moved([(count_in, count), (vert_in, vert), (ctx_in, ctx)], sems)
    lists = moved([(pos_in, pos), (neg_in, neg)], sems, 3)
    loads = moved([(context, c_old), (vertex, v_old)], sems, 5)
    waited(heads)
    mine = choose(chosen, count[0], lambda t: True)
    waited(lists)
    lane = lax.broadcasted_iota(jnp.int32, (8, 128), 1)
    for s in range(1, steps):
        base = LISTED * (s - 1)
        for side in (0, 1):
            lanes = slice(128 * side, 128 * side + 128)
            at = base + SIDE * side
            own[at : at + 8, :] = pos[s, :, lanes].astype(jnp.float32)
            for t in range(SLOTS):
                rows = slice(at + 8 + NEG * t, at + 8 + NEG * t + NEG)
                own[rows, :] = neg[s, t, :, lanes].astype(jnp.float32)
        meta = jnp.where(lane == 16, count[s], 0)
        for t in range(SLOTS):
            meta = jnp.where(lane == t, vert[s, t], meta)
            meta = jnp.where(lane == 8 + t, ctx[s, t], meta)
        meta = meta.astype(jnp.float32)
        own[base + META : base + SIDE, :] = meta
        own[base + SIDE + META : base + LISTED, :] = meta
    waited(loads)

    def fill(n, carry):
        c_new[tile(n), :] = c_old[tile(n), :]
        v_new[tile(2 * n), :] = v_old[tile(2 * n), :]
        v_new[tile(2 * n + 1), :] = v_old[tile(2 * n + 1), :]
        return carry

    lax.fori_loop(0, CTX_TILES, fill, 0)

    def one(t, live):
        vi, ci = vert[0, t], ctx[0, t]
        rows = [neg[0, t, pl.ds(k, 1), :] for k in range(NEG)]
        pos_row = pos[0, pl.ds(t, 1), :]
        dv, dc = slot_update(v_old[tile(vi), :], c_old[tile(ci), :], pos_row, rows, live)
        return v_new, vi, dv, c_new, ci, dc

    run_pairs(chosen, mine, one)
    odd = group_odd()

    @pl.when(odd == 0)
    def even_group():
        stores = [
            (v_new.at[pl.ds(0, HALF)], low_out),
            (v_new.at[pl.ds(HALF, HALF)], high_out),
            (c_new, ctx_out),
            (own, own_out),
        ]
        waited(moved(stores, sems))

    @pl.when(odd == 1)
    def odd_group():
        stores = [
            (c_new.at[pl.ds(0, QUARTER)], moved_out.at[pl.ds(0, QUARTER)]),
            (own, moved_out.at[pl.ds(QUARTER, LISTED * (steps - 1))]),
            (c_new.at[pl.ds(QUARTER, QUARTER)], moved_high),
            (v_new, vert_out),
        ]
        waited(moved(stores, sems))


def first_step(vertex, context, lists):
    steps = lists[0].shape[0]
    listed = LISTED * (steps - 1)

    def kernel(*refs):
        first_kernel(steps, *refs)

    return pl.pallas_call(
        kernel,
        out_shape=[
            wide(HALF),
            wide(HALF),
            wide(QUARTER + listed),
            wide(QUARTER),
            wide(HALF),
            wide(2 * HALF),
            wide(listed),
        ],
        in_specs=[ANY] * 7,
        out_specs=[ANY] * 7,
        scratch_shapes=[
            vmem(2 * HALF),
            vmem(2 * HALF),
            vmem(HALF),
            vmem(HALF),
            pltpu.SMEM((steps,), jnp.int32),
            pltpu.SMEM((steps, SLOTS), jnp.int32),
            pltpu.SMEM((steps, SLOTS), jnp.int32),
            pltpu.VMEM((steps, SLOTS, TILE), jnp.int32),
            pltpu.VMEM((steps, SLOTS, NEG, TILE), jnp.int32),
            vmem(listed),
            pltpu.SMEM((SLOTS + 1,), jnp.int32),
            pltpu.SemaphoreType.DMA((7,)),
        ],
        compiler_params=pltpu.CompilerParams(vmem_limit_bytes=FIRST_LIMIT),
        cost_estimate=pl.CostEstimate(flops=1000, bytes_accessed=1000, transcendentals=0),
    )(vertex, context, *lists)


def head(meta, lane):
    return meta[0, lane].astype(jnp.int32)


def listed_rows(listed, t):
    def row(r):
        both = [listed[pl.ds(r, 1), :], listed[pl.ds(SIDE + r, 1), :]]
        return jnp.concatenate(both, axis=1).astype(jnp.int32)

    return row(t), [row(8 + NEG * t + k) for k in range(NEG)]


def even_kernel(s, half, joined, swaps, n_after, *refs):
    move_in, stay_in, *refs = refs
    total_in = stay_in
    if joined:
        total_in, *refs = refs
    own, *refs = refs
    if swaps:
        give, *refs = refs
    move_out, stay_out, *refs = refs[n_after:]
    m_old, m_new, s_old, s_new, listed, meta, chosen, sems = refs
    if swaps:

        @pl.when(group_odd() == 1)
        def hand_on():
            waited(moved([(give, move_out)], sems))

    @pl.when(group_odd() == 0)
    def work():
        list_in = own.at[pl.ds(LISTED * (s - 1), LISTED)]
        heads = moved([(list_in.at[pl.ds(META, 8)], meta)], sems)
        loads = [
            (list_in, listed),
            (move_in, m_old),
            (stay_in, s_old),
            (move_in, m_new),
            (total_in, s_new),
        ]
        loads = moved(loads, sems, 1)
        waited(heads)
        mine = choose(chosen, head(meta, 16), lambda t: head(meta, t) // 8 == half)
        waited(loads)

        def one(t, live):
            vi, ci = lax.rem(head(meta, t), 8), head(meta, 8 + t)
            rows = listed_rows(listed, t)
            dv, dc = slot_update(m_old[tile(vi), :], s_old[tile(ci), :], *rows, live)
            return m_new, vi, dv, s_new, ci, dc

        run_pairs(chosen, mine, one)
        stores = [(m_new, move_out.at[pl.ds(0, HALF)]), (s_new, stay_out)]
        waited(moved(stores, sems))


def even_step(s, half, moving, staying, total, own, give, after):
    swaps = give is not None
    operands = [moving, staying] + ([] if total is None else [total]) + [own]
    operands += ([give] if swaps else []) + [*after]
    size = give.shape[0] if swaps else HALF

    def kernel(*refs):
        even_kernel(s, half, total is not None, swaps, len(after), *refs)

    return pl.pallas_call(
        kernel,
        out_shape=[wide(size), wide(HALF)],
        in_specs=[ANY] * len(operands),
        out_specs=[ANY, ANY],
        scratch_shapes=[
            vmem(HALF),
            vmem(HALF),
            vmem(HALF),
            vmem(HALF),
            vmem(LISTED),
            pltpu.SMEM((8, 128), jnp.float32),
            pltpu.SMEM((SLOTS + 1,), jnp.int32),
            pltpu.SemaphoreType.DMA((6,)),
        ],
        compiler_params=pltpu.CompilerParams(vmem_limit_bytes=STEP_LIMIT),
        cost_estimate=pl.CostEstimate(flops=1000, bytes_accessed=1000, transcendentals=0),
    )(*operands)


def part_tiles(meta, used, order):
    for n in range(VERT_TILES):
        used[n] = 0
    for t in range(SLOTS):
        at = head(meta, t)
        used[at] = jnp.where(t < head(meta, 16), 1, used[at])
    early, late = jnp.int32(0), jnp.int32(SLOTS)
    for n in range(VERT_TILES):
        soon = (used[n] == 0) & (early < SLOTS)
        order[jnp.where(soon, early, late)] = n
        early = early + soon.astype(jnp.int32)
        late = late + 1 - soon.astype(jnp.int32)


def odd_kernel(left, half, n_after, *refs):
    move_in, stay_in, *refs = refs
    list_in, total_in = move_in.at[pl.ds(QUARTER, LISTED)] if not half else None, stay_in
    parts = left == 0
    if half:
        carrier, total_in, *refs = refs
        list_in = carrier.at[pl.ds(QUARTER, LISTED)]
    joins = half and left == 0
    if joins:
        low_half, *refs = refs
    refs = refs[n_after:]
    move_out, *refs = refs
    if left or not half:
        stay_out, *refs = refs
    if parts:
        part_out, *refs = refs
    m_old, m_new, s_old, s_new, listed, meta, chosen, used, order, places, sems = refs

    @pl.when(group_odd() == 1)
    def work():
        heads = moved([(list_in.at[pl.ds(META, 8)], meta)], sems)
        loads = [
            (list_in, listed),
            (move_in.at[pl.ds(0, QUARTER)], m_old),
            (stay_in, s_old),
            (move_in.at[pl.ds(0, QUARTER)], m_new),
            (total_in, s_new),
        ]
        if left and not half:
            rest = pl.ds(QUARTER, LISTED * left)
            loads.append((move_in.at[pl.ds(QUARTER + LISTED, LISTED * left)], move_out.at[rest]))
        if joins:
            loads.append((low_half, move_out.at[pl.ds(0, QUARTER)]))
        loads = moved(loads, sems, 2)
        waited(heads)
        mine = choose(chosen, head(meta, 16), lambda t: head(meta, 8 + t) // 4 == half)
        if parts:
            part_tiles(meta, used, order)
        waited(loads)

        def one(t, live):
            vi, ci = head(meta, t), lax.rem(head(meta, 8 + t), 4)
            rows = listed_rows(listed, t)
            dv, dc = slot_update(s_old[tile(vi), :], m_old[tile(ci), :], *rows, live)
            return s_new, vi, dv, m_new, ci, dc

        run_pairs(chosen, mine, one)
        stores = [(m_new, move_out.at[pl.ds(QUARTER if joins else 0, QUARTER)])]
        if left or not half:
            stores.append((s_new, stay_out))
        if parts:
            first = SLOTS if half else 0
            stores += [
                (s_new.at[tile(order[first + n])], part_out.at[pl.ds(n * TILE, TILE)])
                for n in range(SLOTS)
            ]
        if parts and half:
            lane = lax.broadcasted_iota(jnp.int32, (8, 128), 1)
            spot = jnp.zeros((8, 128), jnp.int32)
            for n in range(VERT_TILES):
                spot = jnp.where(lane == n, order[n], spot)
            places[...] = spot.astype(jnp.float32)
            stores.append((places, part_out.at[pl.ds(HALF, 8)]))
            stores.append((places, move_out.at[pl.ds(HALF, 8)]))
        waited(moved(stores, sems))


def odd_step(left, half, moving, staying, carrier, total, low, after):
    operands = [moving, staying]
    joins = half and left == 0
    out_shape = [wide(HALF + 8 if joins else QUARTER + (0 if half else LISTED * left))]
    if left or not half:
        out_shape.append(wide(2 * HALF))
    if half:
        operands += [carrier, total]
    if joins:
        operands.append(low)
    if left == 0:
        out_shape.append(wide(HALF + 8 if half else HALF))

    def kernel(*refs):
        odd_kernel(left, half, len(after), *refs)

    return pl.pallas_call(
        kernel,
        out_shape=out_shape,
        in_specs=[ANY] * (len(operands) + len(after)),
        out_specs=[ANY] * len(out_shape),
        scratch_shapes=[
            vmem(QUARTER),
            vmem(QUARTER),
            vmem(2 * HALF),
            vmem(2 * HALF),
            vmem(LISTED),
            pltpu.SMEM((8, 128), jnp.float32),
            pltpu.SMEM((SLOTS + 1,), jnp.int32),
            pltpu.SMEM((VERT_TILES,), jnp.int32),
            pltpu.SMEM((VERT_TILES,), jnp.int32),
            vmem(8),
            pltpu.SemaphoreType.DMA((13,)),
        ],
        compiler_params=pltpu.CompilerParams(vmem_limit_bytes=STEP_LIMIT),
        cost_estimate=pl.CostEstimate(flops=16000000000, bytes_accessed=1000, transcendentals=0),
    )(*operands, *after)


def finish_kernel(first, second, late, stayed, home, vertex, context, spots, sems):
    odd = group_odd()

    @pl.when(odd == 0)
    def even_group():
        heads = moved([(late.at[pl.ds(HALF, 8)], spots)], sems)
        kept = moved([(stayed, context)], sems, 1)
        waited(heads)
        copies = []
        for n in range(VERT_TILES):
            source = second if n < SLOTS else late
            rows = pl.ds(n % SLOTS * TILE, TILE)
            copies.append((source.at[rows], vertex.at[tile(head(spots, n))]))
        waited(moved(copies, sems, 2))
        waited(kept)

    @pl.when(odd == 1)
    def odd_group():
        copies = [
            (first, vertex.at[pl.ds(0, HALF)]),
            (second, vertex.at[pl.ds(HALF, HALF)]),
            (home.at[pl.ds(0, HALF)], context),
        ]
        waited(moved(copies, sems))


def finish(*operands):
    return pl.pallas_call(
        finish_kernel,
        out_shape=[wide(2 * HALF), wide(HALF)],
        in_specs=[ANY] * 5,
        out_specs=[HBM, HBM],
        scratch_shapes=[
            pltpu.SMEM((8, 128), jnp.float32),
            pltpu.SemaphoreType.DMA((2 + VERT_TILES,)),
        ],
        compiler_params=pltpu.CompilerParams(vmem_limit_bytes=1024 * 1024),
    )(*operands)


def body(vertex, context, *lists):
    groups, members = lax.axis_size("outer"), lax.axis_size("inner")
    steps = lists[0].shape[0]

    def sent(array, odd, move):
        return lax.ppermute(array, AXES, route(groups, members, odd, move))

    low, high, *o, c_state, v_state, own = first_step(vertex, context, lists)
    e = [sent(low, 0, (0, 1)), sent(high, 0, (0, 1))]
    o = [sent(x, 1, (0, -1)) for x in o]

    def even_half(s, h, total, give=None, *after):
        x, total = even_step(s, h, e[h], c_state, total, own, give, after)
        if s + 1 < steps:
            e[h] = sent(x, 0, (0, 1))
        elif give is None:
            e[h] = sent(x, 0, (1, 0))
        else:
            swap = route(groups, members, 0, (1, 0)) + route(groups, members, 1, (-1, 0))
            e[h] = lax.ppermute(x, AXES, swap)
        return total

    def odd_half(s, h, total, *after):
        carrier = None if h == 0 else carriers[s]
        carriers[s] = o[h] if h == 0 else carrier
        x, *rest = odd_step(steps - 1 - s, h, o[h], v_state, carrier, total, o[0], after)
        if s + 1 < steps:
            o[h] = sent(x, 1, (0, -1))
        else:
            o[h] = sent(x, 1, (0, steps - 1)) if h else x
        return rest

    carriers = {}
    beside = (2, steps - 1)
    total = even_half(1, 0, None)
    c_state = even_half(1, 1, total)
    total = even_half(2, 0, None)
    c_state = even_half(2, 1, total)
    (v_state,) = odd_half(1, 1, *odd_half(1, 0, None))
    (v_state,) = odd_half(2, 1, *odd_half(2, 0, None))
    total, early = odd_half(3, 0, None)
    early = sent(early, 1, beside)
    (late,) = odd_half(3, 1, total)
    total = even_half(3, 0, None, None, late)
    late = sent(late, 1, (1, steps - 1))
    c_state = even_half(3, 1, total, early)
    return tuple(finish(*e, late, c_state, o[1]))


def solution(mesh):
    return jax.shard_map(
        body,
        mesh=mesh,
        in_specs=(
            P(AXES, None),
            P(AXES, None),
            P(AXES),
            P(AXES, None),
            P(AXES, None),
            P(AXES, None, None),
            P(AXES, None, None, None),
        ),
        out_specs=(P(AXES, None), P(AXES, None)),
        check_vma=False,
    )
```

```python
import jax
import jax.numpy as jnp
from jax import lax
from jax.experimental import pallas as pl
from jax.experimental.pallas import tpu as pltpu
from jax.sharding import PartitionSpec as P

TILE = 256
WIDTH = 128
SLOTS = 8
NEG = 4
AXES = ("outer", "inner")
META = 40
SIDE = 48
LISTED = 96
VERT_TILES = 16
CTX_TILES = 8
HALF = 8 * TILE
QUARTER = 4 * TILE
FIRST_LIMIT = 60 * 1024 * 1024
STEP_LIMIT = 20 * 1024 * 1024

ANY = pl.BlockSpec(memory_space=pl.ANY)
HBM = pl.BlockSpec(memory_space=pltpu.HBM)


def route(groups, members, odd, move):
    pairs = []
    for o in range(odd, groups, 2):
        for i in range(members):
            to = ((o + move[0]) % groups) * members + (i + move[1]) % members
            pairs.append((o * members + i, to))
    return pairs


def wide(rows):
    return jax.ShapeDtypeStruct((rows, WIDTH), jnp.float32)


def vmem(rows):
    return pltpu.VMEM((rows, WIDTH), jnp.float32)


def tile(n):
    return pl.ds(pl.multiple_of(n * TILE, TILE), TILE)


def started(copies):
    for copy in copies:
        copy.start()
    return copies


def waited(copies):
    for copy in copies:
        copy.wait()


def moved(pairs, sems, first=0):
    return started(
        [
            pltpu.make_async_copy(source, to, sems.at[first + n])
            for n, (source, to) in enumerate(pairs)
        ]
    )


def halves(x):
    high = x.astype(jnp.bfloat16)
    return high, (x - high.astype(jnp.float32)).astype(jnp.bfloat16)


def dot(a, b, dims):
    return lax.dot_general(a, b, (dims, ((), ())), preferred_element_type=jnp.float32)


def slot_update(v, c, pos_row, neg_rows, live):
    v_hi, v_lo = halves(v)
    c_hi, c_lo = halves(c)
    c_both = jnp.concatenate([c_hi, c_lo], axis=1)
    v_both = jnp.concatenate([v_hi, v_lo], axis=1)
    scores = dot(
        jnp.concatenate([c_hi, c_lo, c_hi], axis=1),
        jnp.concatenate([v_hi, v_hi, v_lo], axis=1),
        ((1,), (1,)),
    )
    column = lax.broadcasted_iota(jnp.int32, (TILE, TILE), 0)
    at_pos = pos_row == column
    quarter = jnp.where(live, -0.25, 0.0)
    scale = jnp.where(at_pos, quarter, 0.0)
    for row in neg_rows:
        scale = scale + jnp.where(row == column, quarter, 0.0)
    grad = scale * jnp.tanh(0.5 * scores) + (scale + jnp.where(at_pos, -2.0 * quarter, 0.0))
    g_hi, g_lo = halves(grad)
    dc = dot(
        jnp.concatenate([g_hi, g_lo], axis=1),
        jnp.concatenate([v_both, v_both], axis=0),
        ((1,), (0,)),
    )
    dv = dot(
        jnp.concatenate([g_hi, g_lo], axis=0),
        jnp.concatenate([c_both, c_both], axis=0),
        ((0,), (0,)),
    )
    return dv[:, :WIDTH] + dv[:, WIDTH:], dc[:, :WIDTH] + dc[:, WIDTH:]


def choose(chosen, count, here):
    mine = jnp.int32(0)
    for t in range(SLOTS):
        chosen[mine] = t
        mine = mine + ((t < count) & here(t)).astype(jnp.int32)
    return mine


def run_pairs(chosen, mine, one):
    def pair(n, carry):
        results = []
        for at in (2 * n, 2 * n + 1):
            live = at < mine
            results.append(one(chosen[jnp.where(live, at, 0)], live))
        for v_to, vi, dv, c_to, ci, dc in results:
            v_to[tile(vi), :] += dv
            c_to[tile(ci), :] += dc
        return carry

    lax.fori_loop(0, (mine + 1) // 2, pair, 0)


def group_odd():
    return lax.rem(lax.axis_index("outer"), 2)


def first_kernel(steps, *refs):
    vertex, context, count_in, vert_in, ctx_in, pos_in, neg_in, *refs = refs
    low_out, high_out, moved_out, moved_high, ctx_out, vert_out, own_out, *refs = refs
    v_old, v_new, c_old, c_new, count, vert, ctx, pos, neg, own, chosen, sems = refs
    heads = moved([(count_in, count), (vert_in, vert), (ctx_in, ctx)], sems)
    lists = moved([(pos_in, pos), (neg_in, neg)], sems, 3)
    loads = moved([(context, c_old), (vertex, v_old)], sems, 5)
    waited(heads)
    mine = choose(chosen, count[0], lambda t: True)
    waited(lists)
    lane = lax.broadcasted_iota(jnp.int32, (8, 128), 1)
    for s in range(1, steps):
        base = LISTED * (s - 1)
        for side in (0, 1):
            lanes = slice(128 * side, 128 * side + 128)
            at = base + SIDE * side
            own[at : at + 8, :] = pos[s, :, lanes].astype(jnp.float32)
            for t in range(SLOTS):
                rows = slice(at + 8 + NEG * t, at + 8 + NEG * t + NEG)
                own[rows, :] = neg[s, t, :, lanes].astype(jnp.float32)
        meta = jnp.where(lane == 16, count[s], 0)
        for t in range(SLOTS):
            meta = jnp.where(lane == t, vert[s, t], meta)
            meta = jnp.where(lane == 8 + t, ctx[s, t], meta)
        meta = meta.astype(jnp.float32)
        own[base + META : base + SIDE, :] = meta
        own[base + SIDE + META : base + LISTED, :] = meta
    waited(loads)

    def fill(n, carry):
        c_new[tile(n), :] = c_old[tile(n), :]
        v_new[tile(2 * n), :] = v_old[tile(2 * n), :]
        v_new[tile(2 * n + 1), :] = v_old[tile(2 * n + 1), :]
        return carry

    lax.fori_loop(0, CTX_TILES, fill, 0)

    def one(t, live):
        vi, ci = vert[0, t], ctx[0, t]
        rows = [neg[0, t, pl.ds(k, 1), :] for k in range(NEG)]
        pos_row = pos[0, pl.ds(t, 1), :]
        dv, dc = slot_update(v_old[tile(vi), :], c_old[tile(ci), :], pos_row, rows, live)
        return v_new, vi, dv, c_new, ci, dc

    odd = group_odd()
    kept = pltpu.make_async_copy(own, own_out, sems.at[5])
    sent = pltpu.make_async_copy(
        own, moved_out.at[pl.ds(QUARTER, LISTED * (steps - 1))], sems.at[6]
    )
    kept.start()
    sent.start()
    run_pairs(chosen, mine, one)
    kept.wait()
    sent.wait()

    @pl.when(odd == 0)
    def even_group():
        stores = [
            (v_new.at[pl.ds(0, HALF)], low_out),
            (v_new.at[pl.ds(HALF, HALF)], high_out),
            (c_new, ctx_out),
        ]
        waited(moved(stores, sems))

    @pl.when(odd == 1)
    def odd_group():
        stores = [
            (c_new.at[pl.ds(0, QUARTER)], moved_out.at[pl.ds(0, QUARTER)]),
            (c_new.at[pl.ds(QUARTER, QUARTER)], moved_high),
            (v_new, vert_out),
        ]
        waited(moved(stores, sems))


def first_step(vertex, context, lists):
    steps = lists[0].shape[0]
    listed = LISTED * (steps - 1)

    def kernel(*refs):
        first_kernel(steps, *refs)

    return pl.pallas_call(
        kernel,
        out_shape=[
            wide(HALF),
            wide(HALF),
            wide(QUARTER + listed),
            wide(QUARTER),
            wide(HALF),
            wide(2 * HALF),
            wide(listed),
        ],
        in_specs=[ANY] * 7,
        out_specs=[ANY] * 7,
        scratch_shapes=[
            vmem(2 * HALF),
            vmem(2 * HALF),
            vmem(HALF),
            vmem(HALF),
            pltpu.SMEM((steps,), jnp.int32),
            pltpu.SMEM((steps, SLOTS), jnp.int32),
            pltpu.SMEM((steps, SLOTS), jnp.int32),
            pltpu.VMEM((steps, SLOTS, TILE), jnp.int32),
            pltpu.VMEM((steps, SLOTS, NEG, TILE), jnp.int32),
            vmem(listed),
            pltpu.SMEM((SLOTS + 1,), jnp.int32),
            pltpu.SemaphoreType.DMA((7,)),
        ],
        compiler_params=pltpu.CompilerParams(vmem_limit_bytes=FIRST_LIMIT),
        cost_estimate=pl.CostEstimate(flops=1000, bytes_accessed=1000, transcendentals=0),
    )(vertex, context, *lists)


def head(meta, lane):
    return meta[0, lane].astype(jnp.int32)


def listed_rows(listed, t):
    def row(r):
        both = [listed[pl.ds(r, 1), :], listed[pl.ds(SIDE + r, 1), :]]
        return jnp.concatenate(both, axis=1).astype(jnp.int32)

    return row(t), [row(8 + NEG * t + k) for k in range(NEG)]


def even_kernel(s, half, joined, swaps, n_after, *refs):
    move_in, stay_in, *refs = refs
    total_in = stay_in
    if joined:
        total_in, *refs = refs
    own, *refs = refs
    if swaps:
        give, *refs = refs
    move_out, stay_out, *refs = refs[n_after:]
    m_old, m_new, s_old, s_new, listed, meta, chosen, sems = refs
    if swaps:

        @pl.when(group_odd() == 1)
        def hand_on():
            waited(moved([(give, move_out)], sems))

    @pl.when(group_odd() == 0)
    def work():
        list_in = own.at[pl.ds(LISTED * (s - 1), LISTED)]
        heads = moved([(list_in.at[pl.ds(META, 8)], meta)], sems)
        loads = [
            (list_in, listed),
            (move_in, m_old),
            (stay_in, s_old),
            (move_in, m_new),
            (total_in, s_new),
        ]
        loads = moved(loads, sems, 1)
        waited(heads)
        mine = choose(chosen, head(meta, 16), lambda t: head(meta, t) // 8 == half)
        waited(loads)

        def one(t, live):
            vi, ci = lax.rem(head(meta, t), 8), head(meta, 8 + t)
            rows = listed_rows(listed, t)
            dv, dc = slot_update(m_old[tile(vi), :], s_old[tile(ci), :], *rows, live)
            return m_new, vi, dv, s_new, ci, dc

        run_pairs(chosen, mine, one)
        stores = [(m_new, move_out.at[pl.ds(0, HALF)]), (s_new, stay_out)]
        waited(moved(stores, sems))


def even_step(s, half, moving, staying, total, own, give, after):
    swaps = give is not None
    operands = [moving, staying] + ([] if total is None else [total]) + [own]
    operands += ([give] if swaps else []) + [*after]
    size = give.shape[0] if swaps else HALF

    def kernel(*refs):
        even_kernel(s, half, total is not None, swaps, len(after), *refs)

    return pl.pallas_call(
        kernel,
        out_shape=[wide(size), wide(HALF)],
        in_specs=[ANY] * len(operands),
        out_specs=[ANY, ANY],
        scratch_shapes=[
            vmem(HALF),
            vmem(HALF),
            vmem(HALF),
            vmem(HALF),
            vmem(LISTED),
            pltpu.SMEM((8, 128), jnp.float32),
            pltpu.SMEM((SLOTS + 1,), jnp.int32),
            pltpu.SemaphoreType.DMA((6,)),
        ],
        compiler_params=pltpu.CompilerParams(vmem_limit_bytes=STEP_LIMIT),
        cost_estimate=pl.CostEstimate(flops=4000000000, bytes_accessed=1000, transcendentals=0),
    )(*operands)


def part_tiles(meta, used, order):
    for n in range(VERT_TILES):
        used[n] = 0
    for t in range(SLOTS):
        at = head(meta, t)
        used[at] = jnp.where(t < head(meta, 16), 1, used[at])
    early, late = jnp.int32(0), jnp.int32(SLOTS)
    for n in range(VERT_TILES):
        soon = (used[n] == 0) & (early < SLOTS)
        order[jnp.where(soon, early, late)] = n
        early = early + soon.astype(jnp.int32)
        late = late + 1 - soon.astype(jnp.int32)


def odd_kernel(left, half, n_after, *refs):
    move_in, stay_in, *refs = refs
    list_in, total_in = move_in.at[pl.ds(QUARTER, LISTED)] if not half else None, stay_in
    parts = left == 0
    if half:
        carrier, total_in, *refs = refs
        list_in = carrier.at[pl.ds(QUARTER, LISTED)]
    joins = half and left == 0
    if joins:
        low_half, *refs = refs
    refs = refs[n_after:]
    move_out, *refs = refs
    if left or not half:
        stay_out, *refs = refs
    if parts:
        part_out, *refs = refs
    m_old, m_new, s_old, s_new, listed, meta, chosen, used, order, places, sems = refs

    @pl.when(group_odd() == 1)
    def work():
        heads = moved([(list_in.at[pl.ds(META, 8)], meta)], sems)
        loads = [
            (list_in, listed),
            (move_in.at[pl.ds(0, QUARTER)], m_old),
            (stay_in, s_old),
            (move_in.at[pl.ds(0, QUARTER)], m_new),
            (total_in, s_new),
        ]
        if left and not half:
            rest = pl.ds(QUARTER, LISTED * left)
            loads.append((move_in.at[pl.ds(QUARTER + LISTED, LISTED * left)], move_out.at[rest]))
        if joins:
            loads.append((low_half, move_out.at[pl.ds(0, QUARTER)]))
        loads = moved(loads, sems, 2)
        waited(heads)
        mine = choose(chosen, head(meta, 16), lambda t: head(meta, 8 + t) // 4 == half)
        if parts:
            part_tiles(meta, used, order)
        waited(loads)

        def one(t, live):
            vi, ci = head(meta, t), lax.rem(head(meta, 8 + t), 4)
            rows = listed_rows(listed, t)
            dv, dc = slot_update(s_old[tile(vi), :], m_old[tile(ci), :], *rows, live)
            return s_new, vi, dv, m_new, ci, dc

        run_pairs(chosen, mine, one)
        stores = [(m_new, move_out.at[pl.ds(QUARTER if joins else 0, QUARTER)])]
        if left or not half:
            stores.append((s_new, stay_out))
        if parts:
            first = SLOTS if half else 0
            stores += [
                (s_new.at[tile(order[first + n])], part_out.at[pl.ds(n * TILE, TILE)])
                for n in range(SLOTS)
            ]
        if parts and half:
            lane = lax.broadcasted_iota(jnp.int32, (8, 128), 1)
            spot = jnp.zeros((8, 128), jnp.int32)
            for n in range(VERT_TILES):
                spot = jnp.where(lane == n, order[n], spot)
            places[...] = spot.astype(jnp.float32)
            stores.append((places, part_out.at[pl.ds(HALF, 8)]))
            stores.append((places, move_out.at[pl.ds(HALF, 8)]))
        waited(moved(stores, sems))


def odd_step(left, half, moving, staying, carrier, total, low, after):
    operands = [moving, staying]
    joins = half and left == 0
    out_shape = [wide(HALF + 8 if joins else QUARTER + (0 if half else LISTED * left))]
    if left or not half:
        out_shape.append(wide(2 * HALF))
    if half:
        operands += [carrier, total]
    if joins:
        operands.append(low)
    if left == 0:
        out_shape.append(wide(HALF + 8 if half else HALF))

    def kernel(*refs):
        odd_kernel(left, half, len(after), *refs)

    return pl.pallas_call(
        kernel,
        out_shape=out_shape,
        in_specs=[ANY] * (len(operands) + len(after)),
        out_specs=[ANY] * len(out_shape),
        scratch_shapes=[
            vmem(QUARTER),
            vmem(QUARTER),
            vmem(2 * HALF),
            vmem(2 * HALF),
            vmem(LISTED),
            pltpu.SMEM((8, 128), jnp.float32),
            pltpu.SMEM((SLOTS + 1,), jnp.int32),
            pltpu.SMEM((VERT_TILES,), jnp.int32),
            pltpu.SMEM((VERT_TILES,), jnp.int32),
            vmem(8),
            pltpu.SemaphoreType.DMA((13,)),
        ],
        compiler_params=pltpu.CompilerParams(vmem_limit_bytes=STEP_LIMIT),
        cost_estimate=pl.CostEstimate(flops=2000000000, bytes_accessed=1000, transcendentals=0),
    )(*operands, *after)


def finish_kernel(first, second, late, stayed, home, vertex, context, spots, sems):
    odd = group_odd()

    @pl.when(odd == 0)
    def even_group():
        heads = moved([(late.at[pl.ds(HALF, 8)], spots)], sems)
        kept = moved([(stayed, context)], sems, 1)
        waited(heads)
        copies = []
        for n in range(VERT_TILES):
            source = second if n < SLOTS else late
            rows = pl.ds(n % SLOTS * TILE, TILE)
            copies.append((source.at[rows], vertex.at[tile(head(spots, n))]))
        waited(moved(copies, sems, 2))
        waited(kept)

    @pl.when(odd == 1)
    def odd_group():
        copies = [
            (first, vertex.at[pl.ds(0, HALF)]),
            (second, vertex.at[pl.ds(HALF, HALF)]),
            (home.at[pl.ds(0, HALF)], context),
        ]
        waited(moved(copies, sems))


def finish(*operands):
    return pl.pallas_call(
        finish_kernel,
        out_shape=[wide(2 * HALF), wide(HALF)],
        in_specs=[ANY] * 5,
        out_specs=[HBM, HBM],
        scratch_shapes=[
            pltpu.SMEM((8, 128), jnp.float32),
            pltpu.SemaphoreType.DMA((2 + VERT_TILES,)),
        ],
        compiler_params=pltpu.CompilerParams(vmem_limit_bytes=1024 * 1024),
    )(*operands)


def body(vertex, context, *lists):
    groups, members = lax.axis_size("outer"), lax.axis_size("inner")
    steps = lists[0].shape[0]

    def sent(array, odd, move):
        return lax.ppermute(array, AXES, route(groups, members, odd, move))

    low, high, *o, c_state, v_state, own = first_step(vertex, context, lists)
    e = [sent(low, 0, (0, 1)), sent(high, 0, (0, 1))]
    o = [sent(x, 1, (0, -1)) for x in o]

    def even_half(s, h, total, give=None, *after):
        x, total = even_step(s, h, e[h], c_state, total, own, give, after)
        if s + 1 < steps:
            e[h] = sent(x, 0, (0, 1))
        elif give is None:
            e[h] = sent(x, 0, (1, 0))
        else:
            swap = route(groups, members, 0, (1, 0)) + route(groups, members, 1, (-1, 0))
            e[h] = lax.ppermute(x, AXES, swap)
        return total

    def odd_half(s, h, total, *after):
        carrier = None if h == 0 else carriers[s]
        carriers[s] = o[h] if h == 0 else carrier
        x, *rest = odd_step(steps - 1 - s, h, o[h], v_state, carrier, total, o[0], after)
        if s + 1 < steps:
            o[h] = sent(x, 1, (0, -1))
        else:
            o[h] = sent(x, 1, (0, steps - 1)) if h else x
        return rest

    carriers = {}
    beside = (2, steps - 1)
    total = even_half(1, 0, None)
    c_state = even_half(1, 1, total)
    total = even_half(2, 0, None)
    c_state = even_half(2, 1, total)
    (v_state,) = odd_half(1, 1, *odd_half(1, 0, None))
    (v_state,) = odd_half(2, 1, *odd_half(2, 0, None))
    total, early = odd_half(3, 0, None)
    early = sent(early, 1, beside)
    (late,) = odd_half(3, 1, total)
    total = even_half(3, 0, None, None, late)
    late = sent(late, 1, (1, steps - 1))
    c_state = even_half(3, 1, total, early)
    return tuple(finish(*e, late, c_state, o[1]))


def solution(mesh):
    return jax.shard_map(
        body,
        mesh=mesh,
        in_specs=(
            P(AXES, None),
            P(AXES, None),
            P(AXES),
            P(AXES, None),
            P(AXES, None),
            P(AXES, None, None),
            P(AXES, None, None, None),
        ),
        out_specs=(P(AXES, None), P(AXES, None)),
        check_vma=False,
    )
```

```python
import jax
import jax.numpy as jnp
from jax import lax
from jax.experimental import pallas as pl
from jax.experimental.pallas import tpu as pltpu
from jax.sharding import PartitionSpec as P

TILE = 256
WIDTH = 128
SLOTS = 8
NEG = 4
AXES = ("outer", "inner")
META = 40
SIDE = 48
LISTED = 96
VERT_TILES = 16
CTX_TILES = 8
HALF = 8 * TILE
QUARTER = 4 * TILE
FIRST_LIMIT = 60 * 1024 * 1024
STEP_LIMIT = 20 * 1024 * 1024

ANY = pl.BlockSpec(memory_space=pl.ANY)
HBM = pl.BlockSpec(memory_space=pltpu.HBM)


def route(groups, members, odd, move):
    pairs = []
    for o in range(odd, groups, 2):
        for i in range(members):
            to = ((o + move[0]) % groups) * members + (i + move[1]) % members
            pairs.append((o * members + i, to))
    return pairs


def wide(rows):
    return jax.ShapeDtypeStruct((rows, WIDTH), jnp.float32)


def vmem(rows):
    return pltpu.VMEM((rows, WIDTH), jnp.float32)


def tile(n):
    return pl.ds(pl.multiple_of(n * TILE, TILE), TILE)


def started(copies):
    for copy in copies:
        copy.start()
    return copies


def waited(copies):
    for copy in copies:
        copy.wait()


def moved(pairs, sems, first=0):
    return started(
        [
            pltpu.make_async_copy(source, to, sems.at[first + n])
            for n, (source, to) in enumerate(pairs)
        ]
    )


def halves(x):
    high = x.astype(jnp.bfloat16)
    return high, (x - high.astype(jnp.float32)).astype(jnp.bfloat16)


def dot(a, b, dims):
    return lax.dot_general(a, b, (dims, ((), ())), preferred_element_type=jnp.float32)


def slot_update(v, c, pos_row, neg_rows, live):
    v_hi, v_lo = halves(v)
    c_hi, c_lo = halves(c)
    c_both = jnp.concatenate([c_hi, c_lo], axis=1)
    v_both = jnp.concatenate([v_hi, v_lo], axis=1)
    scores = dot(
        jnp.concatenate([c_hi, c_lo, c_hi], axis=1),
        jnp.concatenate([v_hi, v_hi, v_lo], axis=1),
        ((1,), (1,)),
    )
    column = lax.broadcasted_iota(jnp.int32, (TILE, TILE), 0)
    at_pos = pos_row == column
    quarter = jnp.where(live, -0.25, 0.0)
    scale = jnp.where(at_pos, quarter, 0.0)
    for row in neg_rows:
        scale = scale + jnp.where(row == column, quarter, 0.0)
    grad = scale * jnp.tanh(0.5 * scores) + (scale + jnp.where(at_pos, -2.0 * quarter, 0.0))
    g_hi, g_lo = halves(grad)
    dc = dot(
        jnp.concatenate([g_hi, g_lo], axis=1),
        jnp.concatenate([v_both, v_both], axis=0),
        ((1,), (0,)),
    )
    dv = dot(
        jnp.concatenate([g_hi, g_lo], axis=0),
        jnp.concatenate([c_both, c_both], axis=0),
        ((0,), (0,)),
    )
    return dv[:, :WIDTH] + dv[:, WIDTH:], dc[:, :WIDTH] + dc[:, WIDTH:]


def choose(chosen, count, here):
    mine = jnp.int32(0)
    for t in range(SLOTS):
        chosen[mine] = t
        mine = mine + ((t < count) & here(t)).astype(jnp.int32)
    return mine


def run_pairs(chosen, mine, one):
    def pair(n, carry):
        results = []
        for at in (2 * n, 2 * n + 1):
            live = at < mine
            results.append(one(chosen[jnp.where(live, at, 0)], live))
        for v_to, vi, dv, c_to, ci, dc in results:
            v_to[tile(vi), :] += dv
            c_to[tile(ci), :] += dc
        return carry

    lax.fori_loop(0, (mine + 1) // 2, pair, 0)


def group_odd():
    return lax.rem(lax.axis_index("outer"), 2)


def first_kernel(steps, *refs):
    vertex, context, count_in, vert_in, ctx_in, pos_in, neg_in, *refs = refs
    low_out, high_out, moved_out, moved_high, ctx_out, vert_out, own_out, *refs = refs
    v_old, v_new, c_old, c_new, count, vert, ctx, pos, neg, own, chosen, sems = refs
    heads = moved([(count_in, count), (vert_in, vert), (ctx_in, ctx)], sems)
    lists = moved([(pos_in, pos), (neg_in, neg)], sems, 3)
    loads = moved([(context, c_old), (vertex, v_old)], sems, 5)
    waited(heads)
    mine = choose(chosen, count[0], lambda t: True)
    waited(lists)
    lane = lax.broadcasted_iota(jnp.int32, (8, 128), 1)
    for s in range(1, steps):
        base = LISTED * (s - 1)
        for side in (0, 1):
            lanes = slice(128 * side, 128 * side + 128)
            at = base + SIDE * side
            own[at : at + 8, :] = pos[s, :, lanes].astype(jnp.float32)
            for t in range(SLOTS):
                rows = slice(at + 8 + NEG * t, at + 8 + NEG * t + NEG)
                own[rows, :] = neg[s, t, :, lanes].astype(jnp.float32)
        meta = jnp.where(lane == 16, count[s], 0)
        for t in range(SLOTS):
            meta = jnp.where(lane == t, vert[s, t], meta)
            meta = jnp.where(lane == 8 + t, ctx[s, t], meta)
        meta = meta.astype(jnp.float32)
        own[base + META : base + SIDE, :] = meta
        own[base + SIDE + META : base + LISTED, :] = meta
    waited(loads)

    def fill(n, carry):
        c_new[tile(n), :] = c_old[tile(n), :]
        v_new[tile(2 * n), :] = v_old[tile(2 * n), :]
        v_new[tile(2 * n + 1), :] = v_old[tile(2 * n + 1), :]
        return carry

    lax.fori_loop(0, CTX_TILES, fill, 0)

    def one(t, live):
        vi, ci = vert[0, t], ctx[0, t]
        rows = [neg[0, t, pl.ds(k, 1), :] for k in range(NEG)]
        pos_row = pos[0, pl.ds(t, 1), :]
        dv, dc = slot_update(v_old[tile(vi), :], c_old[tile(ci), :], pos_row, rows, live)
        return v_new, vi, dv, c_new, ci, dc

    odd = group_odd()
    kept = pltpu.make_async_copy(own, own_out, sems.at[5])
    sent = pltpu.make_async_copy(
        own, moved_out.at[pl.ds(QUARTER, LISTED * (steps - 1))], sems.at[6]
    )
    kept.start()
    sent.start()
    run_pairs(chosen, mine, one)
    kept.wait()
    sent.wait()

    @pl.when(odd == 0)
    def even_group():
        stores = [
            (v_new.at[pl.ds(0, HALF)], low_out),
            (v_new.at[pl.ds(HALF, HALF)], high_out),
            (c_new, ctx_out),
        ]
        waited(moved(stores, sems))

    @pl.when(odd == 1)
    def odd_group():
        stores = [
            (c_new.at[pl.ds(0, QUARTER)], moved_out.at[pl.ds(0, QUARTER)]),
            (c_new.at[pl.ds(QUARTER, QUARTER)], moved_high),
            (v_new, vert_out),
        ]
        waited(moved(stores, sems))


def first_step(vertex, context, lists):
    steps = lists[0].shape[0]
    listed = LISTED * (steps - 1)

    def kernel(*refs):
        first_kernel(steps, *refs)

    return pl.pallas_call(
        kernel,
        out_shape=[
            wide(HALF),
            wide(HALF),
            wide(QUARTER + listed),
            wide(QUARTER),
            wide(HALF),
            wide(2 * HALF),
            wide(listed),
        ],
        in_specs=[ANY] * 7,
        out_specs=[ANY] * 7,
        scratch_shapes=[
            vmem(2 * HALF),
            vmem(2 * HALF),
            vmem(HALF),
            vmem(HALF),
            pltpu.SMEM((steps,), jnp.int32),
            pltpu.SMEM((steps, SLOTS), jnp.int32),
            pltpu.SMEM((steps, SLOTS), jnp.int32),
            pltpu.VMEM((steps, SLOTS, TILE), jnp.int32),
            pltpu.VMEM((steps, SLOTS, NEG, TILE), jnp.int32),
            vmem(listed),
            pltpu.SMEM((SLOTS + 1,), jnp.int32),
            pltpu.SemaphoreType.DMA((7,)),
        ],
        compiler_params=pltpu.CompilerParams(vmem_limit_bytes=FIRST_LIMIT),
        cost_estimate=pl.CostEstimate(flops=1000, bytes_accessed=1000, transcendentals=0),
    )(vertex, context, *lists)


def head(meta, lane):
    return meta[0, lane].astype(jnp.int32)


def listed_rows(listed, t):
    def row(r):
        both = [listed[pl.ds(r, 1), :], listed[pl.ds(SIDE + r, 1), :]]
        return jnp.concatenate(both, axis=1).astype(jnp.int32)

    return row(t), [row(8 + NEG * t + k) for k in range(NEG)]


def even_kernel(s, half, joined, swaps, n_after, *refs):
    move_in, stay_in, *refs = refs
    total_in = stay_in
    if joined:
        total_in, *refs = refs
    own, *refs = refs
    if swaps:
        give, *refs = refs
    move_out, stay_out, *refs = refs[n_after:]
    m_old, m_new, s_old, s_new, listed, meta, chosen, sems = refs
    if swaps:

        @pl.when(group_odd() == 1)
        def hand_on():
            waited(moved([(give, move_out)], sems))

    @pl.when(group_odd() == 0)
    def work():
        list_in = own.at[pl.ds(LISTED * (s - 1), LISTED)]
        heads = moved([(list_in.at[pl.ds(META, 8)], meta)], sems)
        loads = [
            (list_in, listed),
            (move_in, m_old),
            (stay_in, s_old),
            (move_in, m_new),
            (total_in, s_new),
        ]
        loads = moved(loads, sems, 1)
        waited(heads)
        mine = choose(chosen, head(meta, 16), lambda t: head(meta, t) // 8 == half)
        waited(loads)

        def one(t, live):
            vi, ci = lax.rem(head(meta, t), 8), head(meta, 8 + t)
            rows = listed_rows(listed, t)
            dv, dc = slot_update(m_old[tile(vi), :], s_old[tile(ci), :], *rows, live)
            return m_new, vi, dv, s_new, ci, dc

        run_pairs(chosen, mine, one)
        stores = [(m_new, move_out.at[pl.ds(0, HALF)]), (s_new, stay_out)]
        waited(moved(stores, sems))


def even_step(s, half, moving, staying, total, own, give, after):
    swaps = give is not None
    operands = [moving, staying] + ([] if total is None else [total]) + [own]
    operands += ([give] if swaps else []) + [*after]
    size = give.shape[0] if swaps else HALF

    def kernel(*refs):
        even_kernel(s, half, total is not None, swaps, len(after), *refs)

    return pl.pallas_call(
        kernel,
        out_shape=[wide(size), wide(HALF)],
        in_specs=[ANY] * len(operands),
        out_specs=[ANY, ANY],
        scratch_shapes=[
            vmem(HALF),
            vmem(HALF),
            vmem(HALF),
            vmem(HALF),
            vmem(LISTED),
            pltpu.SMEM((8, 128), jnp.float32),
            pltpu.SMEM((SLOTS + 1,), jnp.int32),
            pltpu.SemaphoreType.DMA((6,)),
        ],
        compiler_params=pltpu.CompilerParams(vmem_limit_bytes=STEP_LIMIT),
        cost_estimate=pl.CostEstimate(flops=1000, bytes_accessed=1000, transcendentals=0),
    )(*operands)


def part_tiles(meta, used, order):
    for n in range(VERT_TILES):
        used[n] = 0
    for t in range(SLOTS):
        at = head(meta, t)
        used[at] = jnp.where(t < head(meta, 16), 1, used[at])
    early, late = jnp.int32(0), jnp.int32(SLOTS)
    for n in range(VERT_TILES):
        soon = (used[n] == 0) & (early < SLOTS)
        order[jnp.where(soon, early, late)] = n
        early = early + soon.astype(jnp.int32)
        late = late + 1 - soon.astype(jnp.int32)


def odd_kernel(left, half, n_after, *refs):
    move_in, stay_in, *refs = refs
    list_in, total_in = move_in.at[pl.ds(QUARTER, LISTED)] if not half else None, stay_in
    parts = half and left == 0
    if half:
        carrier, total_in, *refs = refs
        list_in = carrier.at[pl.ds(QUARTER, LISTED)]
    joins = half and left == 0
    if joins:
        low_half, *refs = refs
    refs = refs[n_after:]
    move_out, *refs = refs
    if left or not half:
        stay_out, *refs = refs
    if parts:
        early_out, part_out, *refs = refs
    m_old, m_new, s_old, s_new, listed, meta, chosen, used, order, places, sems = refs

    @pl.when(group_odd() == 1)
    def work():
        heads = moved([(list_in.at[pl.ds(META, 8)], meta)], sems)
        loads = [
            (list_in, listed),
            (move_in.at[pl.ds(0, QUARTER)], m_old),
            (stay_in, s_old),
            (move_in.at[pl.ds(0, QUARTER)], m_new),
            (total_in, s_new),
        ]
        if left and not half:
            rest = pl.ds(QUARTER, LISTED * left)
            loads.append((move_in.at[pl.ds(QUARTER + LISTED, LISTED * left)], move_out.at[rest]))
        if joins:
            loads.append((low_half, move_out.at[pl.ds(0, QUARTER)]))
        loads = moved(loads, sems, 2)
        waited(heads)
        mine = choose(chosen, head(meta, 16), lambda t: head(meta, 8 + t) // 4 == half)
        if parts:
            part_tiles(meta, used, order)
        waited(loads)

        def one(t, live):
            vi, ci = head(meta, t), lax.rem(head(meta, 8 + t), 4)
            rows = listed_rows(listed, t)
            dv, dc = slot_update(s_old[tile(vi), :], m_old[tile(ci), :], *rows, live)
            return s_new, vi, dv, m_new, ci, dc

        run_pairs(chosen, mine, one)
        stores = [(m_new, move_out.at[pl.ds(QUARTER if joins else 0, QUARTER)])]
        if left or not half:
            stores.append((s_new, stay_out))
        if parts:
            for n in range(VERT_TILES):
                out = early_out if n < SLOTS else part_out
                rows = pl.ds(n % SLOTS * TILE, TILE)
                stores.append((s_new.at[tile(order[n])], out.at[rows]))
        if parts and half:
            lane = lax.broadcasted_iota(jnp.int32, (8, 128), 1)
            spot = jnp.zeros((8, 128), jnp.int32)
            for n in range(VERT_TILES):
                spot = jnp.where(lane == n, order[n], spot)
            places[...] = spot.astype(jnp.float32)
            stores.append((places, part_out.at[pl.ds(HALF, 8)]))
            stores.append((places, move_out.at[pl.ds(HALF, 8)]))
        waited(moved(stores, sems))


def odd_step(left, half, moving, staying, carrier, total, low, after):
    operands = [moving, staying]
    joins = half and left == 0
    out_shape = [wide(HALF + 8 if joins else QUARTER + (0 if half else LISTED * left))]
    if left or not half:
        out_shape.append(wide(2 * HALF))
    if half:
        operands += [carrier, total]
    if joins:
        operands.append(low)
    if joins:
        out_shape += [wide(HALF), wide(HALF + 8)]

    def kernel(*refs):
        odd_kernel(left, half, len(after), *refs)

    return pl.pallas_call(
        kernel,
        out_shape=out_shape,
        in_specs=[ANY] * (len(operands) + len(after)),
        out_specs=[ANY] * len(out_shape),
        scratch_shapes=[
            vmem(QUARTER),
            vmem(QUARTER),
            vmem(2 * HALF),
            vmem(2 * HALF),
            vmem(LISTED),
            pltpu.SMEM((8, 128), jnp.float32),
            pltpu.SMEM((SLOTS + 1,), jnp.int32),
            pltpu.SMEM((VERT_TILES,), jnp.int32),
            pltpu.SMEM((VERT_TILES,), jnp.int32),
            vmem(8),
            pltpu.SemaphoreType.DMA((20,)),
        ],
        compiler_params=pltpu.CompilerParams(vmem_limit_bytes=STEP_LIMIT),
        cost_estimate=pl.CostEstimate(flops=16000000000, bytes_accessed=1000, transcendentals=0),
    )(*operands, *after)


def finish_kernel(first, second, late, stayed, home, vertex, context, spots, sems):
    odd = group_odd()

    @pl.when(odd == 0)
    def even_group():
        heads = moved([(late.at[pl.ds(HALF, 8)], spots)], sems)
        kept = moved([(stayed, context)], sems, 1)
        waited(heads)
        copies = []
        for n in range(VERT_TILES):
            source = second if n < SLOTS else late
            rows = pl.ds(n % SLOTS * TILE, TILE)
            copies.append((source.at[rows], vertex.at[tile(head(spots, n))]))
        waited(moved(copies, sems, 2))
        waited(kept)

    @pl.when(odd == 1)
    def odd_group():
        copies = [
            (first, vertex.at[pl.ds(0, HALF)]),
            (second, vertex.at[pl.ds(HALF, HALF)]),
            (home.at[pl.ds(0, HALF)], context),
        ]
        waited(moved(copies, sems))


def finish(*operands):
    return pl.pallas_call(
        finish_kernel,
        out_shape=[wide(2 * HALF), wide(HALF)],
        in_specs=[ANY] * 5,
        out_specs=[HBM, HBM],
        scratch_shapes=[
            pltpu.SMEM((8, 128), jnp.float32),
            pltpu.SemaphoreType.DMA((2 + VERT_TILES,)),
        ],
        compiler_params=pltpu.CompilerParams(vmem_limit_bytes=1024 * 1024),
    )(*operands)


def body(vertex, context, *lists):
    groups, members = lax.axis_size("outer"), lax.axis_size("inner")
    steps = lists[0].shape[0]

    def sent(array, odd, move):
        return lax.ppermute(array, AXES, route(groups, members, odd, move))

    low, high, *o, c_state, v_state, own = first_step(vertex, context, lists)
    e = [sent(low, 0, (0, 1)), sent(high, 0, (0, 1))]
    o = [sent(x, 1, (0, -1)) for x in o]

    def even_half(s, h, total, give=None, *after):
        x, total = even_step(s, h, e[h], c_state, total, own, give, after)
        if s + 1 < steps:
            e[h] = sent(x, 0, (0, 1))
        elif give is None:
            e[h] = sent(x, 0, (1, 0))
        else:
            swap = route(groups, members, 0, (1, 0)) + route(groups, members, 1, (-1, 0))
            e[h] = lax.ppermute(x, AXES, swap)
        return total

    def odd_half(s, h, total, *after):
        carrier = None if h == 0 else carriers[s]
        carriers[s] = o[h] if h == 0 else carrier
        x, *rest = odd_step(steps - 1 - s, h, o[h], v_state, carrier, total, o[0], after)
        if s + 1 < steps:
            o[h] = sent(x, 1, (0, -1))
        else:
            o[h] = sent(x, 1, (0, steps - 1)) if h else x
        return rest

    carriers = {}
    beside = (2, steps - 1)
    total = even_half(1, 0, None)
    c_state = even_half(1, 1, total)
    total = even_half(2, 0, None)
    c_state = even_half(2, 1, total)
    (v_state,) = odd_half(1, 1, *odd_half(1, 0, None))
    (v_state,) = odd_half(2, 1, *odd_half(2, 0, None))
    early, late = odd_half(3, 1, *odd_half(3, 0, None))
    early = sent(early, 1, beside)
    total = even_half(3, 0, None, None, late)
    late = sent(late, 1, (1, steps - 1))
    c_state = even_half(3, 1, total, early)
    return tuple(finish(*e, late, c_state, o[1]))


def solution(mesh):
    return jax.shard_map(
        body,
        mesh=mesh,
        in_specs=(
            P(AXES, None),
            P(AXES, None),
            P(AXES),
            P(AXES, None),
            P(AXES, None),
            P(AXES, None, None),
            P(AXES, None, None, None),
        ),
        out_specs=(P(AXES, None), P(AXES, None)),
        check_vma=False,
    )
```
